32 devices in a mesh: row: 8 (over z, core), col: 4 (over y, x).
Axes of the slice: x: 2, y: 2, z: 4, core: 2. Of those that a mesh axis runs over, the one named last changes fastest.
Arguments:
- matrix: bfloat16 [7, 2048, 14, 1024], P(None, 'row', None, 'col'), may hold values from -1 to 3
- pivots: int32 [2, 256], replicated, may hold values from 256 to 14335, as said below
Outputs:
- factored: bfloat16 [7, 2048, 14, 1024], P(None, 'row', None, 'col')
The draws below stay inside these ranges and needn't reach their ends.
Inputs may be any that keep to these rules, and one draw needn't show every extreme that they name: Within a step s the pivots[s, :] are distinct and lie in (s + 1) * 256 to 14335.
All inputs are finite; a program needn't handle non-finite values.
Results may differ from the reference program's by a relative error of at most 0.0059.
Values may be sent and summed in bfloat16 or wider, within the bound.
No kernel may reach another device: no remote copies, remote signals or barrier semaphores. Data moves between devices by JAX's collectives and lax.ppermute only.
A program may use at most 128 MiB of HBM per device.

```python
import math
import jax
import jax.numpy as jnp
from jax import lax

NB = 256
STEPS = 2
NEWTON = 3
ORDER = 14336
ROW_CYCLES = 7
COL_CYCLES = 14
N_ROW = 8
N_COL = 4


def pivot_table(key):
    tables = []
    for panel_step in range(STEPS):
        key_pick = jax.random.fold_in(key, 101 + panel_step)
        key_order = jax.random.fold_in(key, 211 + panel_step)
        lowest = (panel_step + 1) * NB
        interior = jax.random.permutation(key_pick, ORDER - lowest - 2)[:NB - 2].astype(jnp.int32) + lowest + 1
        values = jnp.concatenate([jnp.array([lowest, ORDER - 1], dtype=jnp.int32), interior])
        shuffle = jax.random.permutation(key_order, NB)
        tables.append(values[shuffle])
    return jnp.stack(tables).astype(jnp.int32)


def draw_pivots(key, part):
    return pivot_table(key)


def draw_matrix(key, part):
    table = pivot_table(key)
    anchor = jnp.arange(ORDER, dtype=jnp.int32)
    sources = []
    for panel_step in range(STEPS):
        upper_rows = panel_step * NB + jnp.arange(NB, dtype=jnp.int32)
        chosen = table[panel_step]
        from_rows = anchor[chosen]
        moved_up = anchor[upper_rows]
        sources.append(from_rows)
        anchor = anchor.at[upper_rows].set(from_rows).at[chosen].set(moved_up)
    source_rows = jnp.concatenate(sources)
    panel_width = STEPS * NB
    key_base = jax.random.fold_in(key, 7)
    key_small = jax.random.fold_in(key, 11)
    key_diag = jax.random.fold_in(key, 17)
    noise_vals = jax.random.uniform(key_base, (ORDER, ORDER), jnp.float32, -1.0, 1.0)
    entries = noise_vals
    diag_vals = jnp.exp(jax.random.uniform(key_diag, (panel_width,), jnp.float32, math.log(1.2), math.log(3.0)))
    column = jnp.arange(ORDER, dtype=jnp.int32)[None, :]
    entries = jnp.where(column < panel_width, 0.4 * entries, entries)
    small_block = jax.random.uniform(key_small, (panel_width, panel_width), jnp.float32, -1.0 / NB, 1.0 / NB)
    entries = entries.at[source_rows, :panel_width].set(small_block)
    entries = entries.at[source_rows, jnp.arange(panel_width, dtype=jnp.int32)].set(diag_vals)
    return entries.astype(jnp.bfloat16).reshape(ROW_CYCLES, ORDER // ROW_CYCLES, COL_CYCLES, ORDER // COL_CYCLES)


def setup_inputs(seed: int = 0) -> dict:
    keys = jax.random.split(jax.random.key(seed), 3)
    matrix = draw_matrix(jax.random.fold_in(keys[2], 71), 0)
    pivots = draw_pivots(jax.random.fold_in(keys[2], 71), 0)
    return dict(matrix=matrix, pivots=pivots)


def newton_inverse(diag_block):
    identity = jnp.eye(diag_block.shape[0], dtype=jnp.float32)
    approx = identity / 3.0
    for _ in range(NEWTON):
        product = jnp.dot(diag_block, approx, precision=lax.Precision.HIGHEST)
        approx = jnp.dot(approx, 2.0 * identity - product, precision=lax.Precision.HIGHEST)
    return approx


def reference(matrix, pivots):
    current = matrix.reshape(ORDER, ORDER)
    all_rows = jnp.arange(ORDER, dtype=jnp.int32)
    for panel_step in range(STEPS):
        first_row = panel_step * NB
        after_row = first_row + NB
        chosen = pivots[panel_step].astype(jnp.int32)
        top_rows = current[first_row:after_row]
        picked = current[chosen]
        current = current.at[first_row:after_row].set(picked).at[chosen].set(top_rows)
        diag_block = current[first_row:after_row, first_row:after_row].astype(jnp.float32)
        inverse = newton_inverse(diag_block)
        below_mask = (all_rows >= after_row)[:, None]
        panel_vals = current[:, first_row:after_row].astype(jnp.float32)
        lower_panel = jnp.where(below_mask, jnp.dot(panel_vals, inverse, precision=lax.Precision.HIGHEST), 0.0).astype(jnp.bfloat16)
        right_mask = (all_rows >= after_row)[None, :]
        upper_rows = jnp.where(right_mask, current[first_row:after_row], jnp.zeros_like(current[first_row:after_row]))

        def update_rows(operands):
            block_vals, lower_block = operands
            change = jnp.dot(lower_block, upper_rows, preferred_element_type=jnp.float32)
            return (block_vals.astype(jnp.float32) - change).astype(jnp.bfloat16)

        blocks_in = current.reshape(ORDER // NB, NB, ORDER)
        lower_blocks = lower_panel.reshape(ORDER // NB, NB, NB)
        current = lax.map(update_rows, (blocks_in, lower_blocks)).reshape(ORDER, ORDER)
        current = current.at[:, first_row:after_row].set(jnp.where(below_mask, lower_panel, current[:, first_row:after_row]))
    return current.reshape(ROW_CYCLES, N_ROW * NB, COL_CYCLES, N_COL * NB)
```

```python
import functools

import jax
import jax.numpy as jnp
from jax import lax
from jax.experimental import pallas as pl
from jax.experimental.pallas import tpu as pltpu
from jax.sharding import PartitionSpec as P

STEPS = 2
NEWTON = 3
CHUNKS = 4
F32 = jnp.float32
BF16 = jnp.bfloat16
VMEM_LIMIT = 56 * 1024 * 1024


def dot(a, b):
    return jnp.dot(a, b, preferred_element_type=F32)


def dot_full(a, b):
    return jnp.dot(a, b, precision=lax.Precision.HIGHEST, preferred_element_type=F32)


def gather_kernel(rows_ref, block_ref, mine_ref, other_ref, onehot):
    cycles, slots, size = onehot.shape

    @pl.when(pl.program_id(0) == 0)
    def _():
        wanted = rows_ref[...]
        for cycle in range(cycles):
            at = lax.broadcasted_iota(jnp.int32, (slots, size), 1) + cycle * size
            onehot[cycle] = jnp.where(wanted == at, 1.0, 0.0).astype(BF16)

    total = dot(onehot[0], block_ref[0, 0])
    for cycle in range(1, cycles):
        total += dot(onehot[cycle], block_ref[cycle, 0])
    mine_ref[0] = total[: slots // 2].astype(BF16)
    other_ref[0] = total[slots // 2 :].astype(BF16)


def gather_rows(matrix, rows, first, count):
    cycles, _, size, _ = matrix.shape
    slots = rows.shape[0]
    half = jax.ShapeDtypeStruct((count, slots // 2, size), BF16)
    half_spec = pl.BlockSpec((1, slots // 2, size), lambda j: (j, 0, 0))
    return pl.pallas_call(
        gather_kernel,
        grid=(count,),
        in_specs=[
            pl.BlockSpec((slots, 1), lambda j: (0, 0)),
            pl.BlockSpec((cycles, 1, size, size), lambda j: (0, j + first, 0, 0)),
        ],
        out_specs=[half_spec, half_spec],
        out_shape=[half, half],
        scratch_shapes=[pltpu.VMEM((cycles, slots, size), BF16)],
        compiler_params=pltpu.CompilerParams(vmem_limit_bytes=VMEM_LIMIT),
        cost_estimate=pl.CostEstimate(
            flops=2 * slots * cycles * size * size * count,
            bytes_accessed=2 * (cycles * size + slots) * size * count,
            transcendentals=0,
        ),
        name="gather_rows",
    )(rows, matrix)


def newton_inverse(diag, identity):
    third = 1.0 / 3.0
    approx = (2.0 * identity - diag * third) * third
    for _ in range(NEWTON - 1):
        approx = dot_full(approx, 2.0 * identity - dot_full(diag, approx))
    return approx


def split_dot(a, b):
    high = b.astype(BF16)
    rest = b - high.astype(F32)
    mid = rest.astype(BF16)
    low = (rest - mid.astype(F32)).astype(BF16)
    return dot(a, low) + dot(a, mid) + dot(a, high)


def whole_rows(place, new_mine, x_other, own_other, me_other):
    new_other = jnp.where(me_other, own_other, x_other)
    first_core = place[1] == 0
    return (
        jnp.where(first_core, new_mine, new_other),
        jnp.where(first_core, new_other, new_mine),
    )


def old_rows(place, x_mine, x_other, top_mine, top_other):
    first_chip = place[0] == 0
    return jnp.concatenate(
        [
            jnp.where(first_chip, top_mine, x_mine),
            jnp.where(first_chip, top_other, x_other),
        ],
        axis=0,
    )


def panel_kernel(
    place, slot_ref, me_ref, panel_ref, new_ref, xm_ref, xo_ref, own_ref, top_ref,
    lower0_ref, lower1_ref, corner_ref, put_ref, keep_ref,
):
    cycles, _, size, _ = panel_ref.shape
    slots = slot_ref.shape[1]
    row = 2 * place[0] + place[1]
    me_other = me_ref[...] != 0
    new0, new1, old = [], [], []
    for b in range(2):
        first, second = whole_rows(place, new_ref[b], xo_ref[b], own_ref[b], me_other)
        new0.append(first)
        new1.append(second)
        old.append(old_rows(place, xm_ref[b], xo_ref[b], panel_ref[0, b], top_ref[b]))
    identity = jnp.where(
        lax.broadcasted_iota(jnp.int32, (size, size), 0)
        == lax.broadcasted_iota(jnp.int32, (size, size), 1),
        1.0,
        0.0,
    ).astype(F32)
    inverse0 = newton_inverse(new0[0].astype(F32), identity)
    corner = split_dot(new1[0], inverse0).astype(BF16)
    corner_ref[...] = corner
    inverse1 = newton_inverse(
        (new1[1].astype(F32) - dot(corner, new0[1])).astype(BF16).astype(F32), identity
    )
    for cycle in range(cycles):
        at = lax.broadcasted_iota(jnp.int32, (size, slots), 0) + cycle * size
        put = jnp.where(slot_ref[...] == at, 1.0, 0.0)
        keep = 1.0 - jnp.sum(put, axis=1, keepdims=True)
        put = put.astype(BF16)
        put_ref[cycle] = put
        keep_ref[cycle] = keep
        left = dot(put, old[0]) + keep * panel_ref[cycle, 0].astype(F32)
        right = dot(put, old[1]) + keep * panel_ref[cycle, 1].astype(F32)
        if cycle == 0:
            left = jnp.where(row == 0, new0[0].astype(F32), jnp.where(row == 1, new1[0].astype(F32), left))
            right = jnp.where(row == 0, new0[1].astype(F32), jnp.where(row == 1, new1[1].astype(F32), right))
        lower = split_dot(left.astype(BF16), inverse0)
        if cycle == 0:
            lower = jnp.where(row == 0, 0.0, lower)
        lower = lower.astype(BF16)
        lower0_ref[cycle] = lower
        right = (right - dot(lower, new0[1])).astype(BF16)
        lower = split_dot(right, inverse1)
        if cycle == 0:
            lower = jnp.where(row <= 1, 0.0, lower)
        lower1_ref[cycle] = lower.astype(BF16)


def factor_panels(place, slot_of, me_other, panel, rows):
    cycles, _, size, _ = panel.shape
    slots = slot_of.shape[1]
    vmem = pl.BlockSpec(memory_space=pltpu.VMEM)
    lower = jax.ShapeDtypeStruct((cycles, size, size), BF16)
    return pl.pallas_call(
        panel_kernel,
        in_specs=[pl.BlockSpec(memory_space=pltpu.SMEM)] + [vmem] * 8,
        out_specs=[vmem] * 5,
        out_shape=[
            lower,
            lower,
            jax.ShapeDtypeStruct((size, size), BF16),
            jax.ShapeDtypeStruct((cycles, size, slots), BF16),
            jax.ShapeDtypeStruct((cycles, size, 1), F32),
        ],
        compiler_params=pltpu.CompilerParams(vmem_limit_bytes=VMEM_LIMIT),
        cost_estimate=pl.CostEstimate(
            flops=8_000_000_000, bytes_accessed=8_000_000, transcendentals=0
        ),
        name="factor_panels",
    )(place, slot_of, me_other, panel, *rows)


def update_kernel(
    first, place, me_ref, block_ref, new_ref, xm_ref, xo_ref, own_ref, top_ref,
    lower0_ref, lower1_ref, corner_ref, put_ref, keep_ref, *rest,
):
    out_ref = rest[-1]
    cycles = lower0_ref.shape[0]
    row = 2 * place[0] + place[1]
    upper0, new1 = whole_rows(place, new_ref[0], xo_ref[0], own_ref[0], me_ref[...] != 0)
    old = old_rows(place, xm_ref[0], xo_ref[0], block_ref[0, 0], top_ref[0])
    upper1 = (new1.astype(F32) - dot(corner_ref[...], upper0)).astype(BF16)
    for cycle in range(cycles):
        block = dot(put_ref[cycle], old) + keep_ref[cycle] * block_ref[cycle, 0].astype(F32)
        if cycle == 0:
            block = jnp.where(row == 0, upper0.astype(F32), jnp.where(row == 1, new1.astype(F32), block))
        block = (block - dot(lower0_ref[cycle], upper0)).astype(BF16).astype(F32)
        out_ref[cycle, 0] = (block - dot(lower1_ref[cycle], upper1)).astype(BF16)
    if first == 0:

        @pl.when(jnp.logical_and(pl.program_id(0) == 0, place[2] == 0))
        def _():
            for cycle in range(cycles):
                block = lower0_ref[cycle]
                if cycle == 0:
                    block = jnp.where(row == 0, upper0, block)
                out_ref[cycle, 0] = block

        @pl.when(jnp.logical_and(pl.program_id(0) == 0, place[2] == 1))
        def _():
            for cycle in range(cycles):
                block = lower1_ref[cycle]
                if cycle == 0:
                    block = jnp.where(row == 0, upper0, jnp.where(row == 1, upper1, block))
                out_ref[cycle, 0] = block


def update_columns(place, me_other, matrix, rows, factors, first, count, result):
    cycles, blocks, size, _ = matrix.shape
    slots = factors[3].shape[2]
    column = pl.BlockSpec((1, slots // 2, size), lambda j: (j, 0, 0))
    whole = lambda a: pl.BlockSpec(a.shape, lambda j, n=a.ndim: (0,) * n)
    blocks_spec = pl.BlockSpec((cycles, 1, size, size), lambda j: (0, j + first, 0, 0))
    operands = [place, me_other, matrix, *rows, *factors]
    in_specs = [pl.BlockSpec(memory_space=pltpu.SMEM), whole(me_other), blocks_spec]
    in_specs += [column] * 4
    in_specs += [pl.BlockSpec((1, size, size), lambda j: (j + first, 0, 0))]
    in_specs += [whole(f) for f in factors]
    aliases = {}
    if result is not None:
        aliases = {len(operands): 0}
        operands.append(result)
        in_specs.append(pl.BlockSpec(memory_space=pl.ANY))
    return pl.pallas_call(
        functools.partial(update_kernel, first),
        grid=(count,),
        in_specs=in_specs,
        out_specs=blocks_spec,
        out_shape=jax.ShapeDtypeStruct(matrix.shape, BF16),
        input_output_aliases=aliases,
        compiler_params=pltpu.CompilerParams(vmem_limit_bytes=VMEM_LIMIT),
        cost_estimate=pl.CostEstimate(
            flops=2 * cycles * size * size * (slots + 2 * size) * count,
            bytes_accessed=4 * cycles * size * size * count,
            transcendentals=0,
        ),
        name="update_columns",
    )(*operands)


def permutation(pivots):
    size = pivots.shape[1]
    index = jnp.arange(size, dtype=jnp.int32)
    pivot0, pivot1 = pivots[0], pivots[1]
    again = pivot0[:, None] == pivot1[None, :]
    inner = pivot0[:, None] == size + index[None, :]
    second = size + index + jnp.sum(jnp.where(inner, index[:, None] - size - index[None, :], 0), 0)
    source1 = pivot1 + jnp.sum(jnp.where(again, index[:, None] - pivot1[None, :], 0), 0)
    leaves0 = index + jnp.sum(jnp.where(again, second[None, :] - index[:, None], 0), 1)
    return jnp.concatenate([pivot0, source1]), jnp.concatenate([leaves0, second])


def send_panels(own, cols):
    col = lax.axis_index("col")
    if cols == 4:
        cross = lax.ppermute(own, "col", [(0, 1), (1, 0)])
        pieces = []
        parts = 2
        step = own.shape[0] // parts if own.shape[0] % parts == 0 else 0
        cuts = [own[i * step : (i + 1) * step] for i in range(parts)] if step else [own]
        for cut in cuts:
            down = lax.ppermute(cut, "col", [(0, 2), (1, 3)])
            over = lax.ppermute(down, "col", [(2, 3), (3, 2)])
            pieces.append((down, over))
        down = jnp.concatenate([p[0] for p in pieces], 0)
        over = jnp.concatenate([p[1] for p in pieces], 0)
        first = jnp.where(col == 0, own, jnp.where(col == 1, cross, jnp.where(col == 2, down, over)))
        second = jnp.where(col == 1, own, jnp.where(col == 0, cross, jnp.where(col == 3, down, over)))
        return first, second
    zero = jnp.zeros_like(own)
    both = jnp.stack([jnp.where(col == 0, own, zero), jnp.where(col == 1, own, zero)])
    both = lax.psum(both, "col")
    return both[0], both[1]


def body(matrix, pivots):
    rows = lax.axis_size("row")
    cols = lax.axis_size("col")
    chips = rows // 2
    row = lax.axis_index("row")
    col = lax.axis_index("col")
    chip = row // 2
    core = row % 2
    cycles, size, blocks, _ = matrix.shape
    slots = STEPS * size
    matrix = matrix.transpose(0, 2, 1, 3)

    source, leaves = permutation(pivots)
    device_of = lambda r: r // size % rows
    local_of = lambda r: r // (size * rows) * size + r % size
    owner = device_of(source) // 2
    me = device_of(source) == row
    from_row = jnp.where(jnp.logical_and(chip == 0, owner != 0), leaves, source)
    taken = jnp.where(device_of(from_row) == row, local_of(from_row), -1)
    outside = jnp.logical_and(me, source >= slots)
    lands = jnp.where(outside, local_of(source), -1)
    absolute = jnp.arange(slots, dtype=jnp.int32)
    lands_top = jnp.max(jnp.where(leaves[None, :] == absolute[:, None], lands[None, :], -1), 1)
    lands = jnp.where(chip == 0, lands_top, lands)
    arrange = lambda v: jnp.where(core == 0, v, jnp.roll(v, size))
    owner = arrange(owner)
    me = arrange(me)
    taken = arrange(taken)[:, None]
    lands = arrange(lands)[None, :]
    me_other = me[size:, None].astype(jnp.int32)
    me_mine = me[None, :size, None]
    owner_mine = owner[None, :size, None]
    place = jnp.stack([chip, core, col]).astype(jnp.int32)

    swap = [(r, r ^ 1) for r in range(rows)]

    def hop_pairs(h):
        pairs = []
        for a, b in ((h, h + 1), (chips - 1 - h, chips - 2 - h)):
            pairs += [(2 * a, 2 * b), (2 * a + 1, 2 * b + 1)]
        return pairs

    def exchange(mine, other):
        native = mine + lax.ppermute(other, "row", swap)
        own = jnp.logical_or(chip == 0, owner_mine == chip)
        received = []
        for h in range(chips - 1):
            out = native if h == 0 else jnp.where(own, native, received[-1])
            received.append(lax.ppermute(out, "row", hop_pairs(h)))
        new = native
        old = native
        for h in range(chips - 1):
            left = jnp.logical_and(chip - 1 == h, owner_mine < chip)
            right = jnp.logical_and(chips - 2 - chip == h, owner_mine > chip)
            new = jnp.where(jnp.logical_or(left, right), received[h], new)
            old = jnp.where(chip - 1 == h, received[h], old)
        theirs = jnp.logical_and(owner_mine == chip, jnp.logical_not(me_mine))
        x_mine = jnp.where(me_mine, old, new)
        x_send = jnp.where(jnp.logical_and(theirs, chip != 0), old, new)
        return new, x_mine, lax.ppermute(x_send, "row", swap), other

    panel_mine, panel_other = gather_rows(matrix, taken, 0, 1)
    native = jnp.concatenate([panel_mine, panel_other], 1)
    native0, native1 = send_panels(native[0], cols)
    raw0, raw1 = send_panels(matrix[:, 0].reshape(cycles * size, size), cols)
    panel = jnp.stack([raw0.reshape(cycles, size, size), raw1.reshape(cycles, size, size)], 1)
    first_swap = [(0, 1), (1, 0)]
    panel_top = lax.ppermute(panel[0], "row", first_swap)
    natives = jnp.stack([native0, native1])
    panel_rows = exchange(natives[:, :size], natives[:, size:])

    top = lax.ppermute(matrix[0], "row", first_swap)
    base, extra = divmod(blocks, CHUNKS)
    counts = [base + (1 if i < extra else 0) for i in range(CHUNKS)]
    starts = [sum(counts[:i]) for i in range(CHUNKS)]
    chunk_rows = []
    for first, count in zip(starts, counts):
        chunk_rows.append(exchange(*gather_rows(matrix, taken, first, count)))

    factors = factor_panels(place, lands, me_other, panel, (*panel_rows, panel_top))
    result = None
    for first, count, chunk in zip(starts, counts, chunk_rows):
        result = update_columns(
            place, me_other, matrix, (*chunk, top), factors, first, count, result
        )
    return result.transpose(0, 2, 1, 3)


def solution(mesh):
    return jax.shard_map(
        body,
        mesh=mesh,
        in_specs=(P(None, "row", None, "col"), P()),
        out_specs=P(None, "row", None, "col"),
        check_vma=False,
    )
```

```python
import functools

import jax
import jax.numpy as jnp
from jax import lax
from jax.experimental import pallas as pl
from jax.experimental.pallas import tpu as pltpu
from jax.sharding import PartitionSpec as P

STEPS = 2
NEWTON = 3
F32 = jnp.float32
BF16 = jnp.bfloat16
I32 = jnp.int32
VMEM_LIMIT = 24 * 1024 * 1024
CHEAP = pl.CostEstimate(flops=1024, bytes_accessed=1024, transcendentals=0)
ANY = pl.BlockSpec(memory_space=pl.ANY)
SMEM = pl.BlockSpec(memory_space=pltpu.SMEM)
VMEM = pl.BlockSpec(memory_space=pltpu.VMEM)


def dot(a, b):
    return jnp.dot(a, b, preferred_element_type=F32)


def dot_full(a, b):
    return jnp.dot(a, b, precision=lax.Precision.HIGHEST, preferred_element_type=F32)


def params():
    return pltpu.CompilerParams(vmem_limit_bytes=VMEM_LIMIT)


def iota(shape, dim):
    return lax.broadcasted_iota(I32, shape, dim)


def to_column(row):
    size = row.shape[1]
    diagonal = iota((size, size), 0) == iota((size, size), 1)
    return jnp.sum(jnp.where(diagonal, row.astype(F32), 0.0), axis=1, keepdims=True).astype(I32)


def to_row(column):
    size = column.shape[0]
    diagonal = iota((size, size), 0) == iota((size, size), 1)
    return jnp.sum(jnp.where(diagonal, column.astype(F32), 0.0), axis=0, keepdims=True).astype(I32)


def pick_sum(mask, value, axis):
    return jnp.sum(jnp.where(mask, value.astype(F32), 0.0), axis=axis, keepdims=True).astype(I32)


def start_kernel(
    rows, place, pivot_ref, block_ref,
    onehot_ref, owner_ref, me_ref, lands_ref, raw_a_ref, raw_b_ref, mine_ref, other_ref, token_ref,
):
    cycles, width, size, _ = block_ref.shape
    chip, core = place[0], place[1]
    row = 2 * chip + core

    @pl.when(pl.program_id(0) == 0)
    def _():
        square = (size, size)
        pivot0, pivot1 = pivot_ref[0:1], pivot_ref[1:2]
        column0 = to_column(pivot0)
        down, across = iota(square, 0), iota(square, 1)
        again = column0 == pivot1
        inner = column0 == across + size
        at = iota((1, size), 1)
        second = size + at + pick_sum(inner, down - across - size, 0)
        source1 = pivot1 + pick_sum(again, down - pivot1, 0)
        leaves0 = iota((size, 1), 0) + pick_sum(again, second - down, 1)
        device_of = lambda r: r // size % rows
        local_of = lambda r: r // (size * rows) * size + r % size

        def of_slots(source, leaves):
            device = device_of(source)
            owner = device // 2
            me = device == row
            come = jnp.where(jnp.logical_and(chip == 0, owner != 0), leaves, source)
            taken = jnp.where(device_of(come) == row, local_of(come), -1)
            return owner, me.astype(I32), taken

        first = of_slots(column0, leaves0)
        last = of_slots(to_column(source1), to_column(second))
        swapped = core == 1
        mine = [jnp.where(swapped, b, a) for a, b in zip(first, last)]
        other = [jnp.where(swapped, a, b) for a, b in zip(first, last)]
        for half, values in enumerate((mine, other)):
            owner_ref[half] = values[0]
            me_ref[half] = values[1]
            for cycle in range(cycles):
                hit = values[2] == across + cycle * size
                onehot_ref[half * size : (half + 1) * size, cycle * size : (cycle + 1) * size] = (
                    jnp.where(hit, 1.0, 0.0).astype(BF16)
                )

        slots = STEPS * size
        lands = []
        for source in (pivot0, source1):
            outside = jnp.logical_and(device_of(source) == row, source >= slots)
            lands.append(jnp.where(outside, local_of(source), -1))
        by_top = []
        leaving = (leaves0, to_column(second))
        landing = [to_column(v) for v in lands]
        for half in range(2):
            total = jnp.full((1, size), -1, I32)
            for leave, land in zip(leaving, landing):
                total += pick_sum(leave == across + half * size, land + 1, 0)
            by_top.append(total)
        lands = [jnp.where(chip == 0, a, b) for a, b in zip(by_top, lands)]
        lands_ref[0:1] = jnp.where(swapped, lands[1], lands[0])
        lands_ref[1:2] = jnp.where(swapped, lands[0], lands[1])
        half = raw_a_ref.shape[0]
        raw_a_ref[...] = block_ref[:half, 0]
        raw_b_ref[...] = block_ref[half:, 0]

    gather_step(onehot_ref, block_ref, mine_ref, other_ref)


def gather_step(onehot_ref, block_ref, mine_ref, other_ref):
    cycles, width, size, _ = block_ref.shape
    columns = [
        jnp.concatenate([block_ref[cycle, b] for cycle in range(cycles)], 0) for b in range(width)
    ]
    columns = columns[0] if width == 1 else jnp.concatenate(columns, 1)
    total = dot(onehot_ref[...], columns).astype(BF16)
    for b in range(width):
        mine_ref[b] = total[:size, b * size : (b + 1) * size]
        other_ref[b] = total[size:, b * size : (b + 1) * size]


def constant(shape):
    return pl.BlockSpec(
        shape, lambda *j, n=len(shape): (0,) * n, pipeline_mode=pl.Buffered(1)
    )


def array(*shape, dtype=BF16):
    return jax.ShapeDtypeStruct(shape, dtype)


TOKEN = array(8, 128, dtype=F32)


def start(place, pivots, matrix, count, width, rows):
    cycles, _, size, _ = matrix.shape
    slots = STEPS * size
    half = (cycles + 1) // 2
    part = array(count, size, size)
    part_spec = pl.BlockSpec((width, size, size), lambda j: (j, 0, 0))
    outs = [
        array(slots, cycles * size),
        array(2, size, 1, dtype=I32),
        array(2, size, 1, dtype=I32),
        array(2, size, dtype=I32),
        array(half, size, size),
        array(cycles - half, size, size),
    ]
    return pl.pallas_call(
        functools.partial(start_kernel, rows),
        grid=(count // width,),
        in_specs=[
            SMEM,
            constant(pivots.shape),
            pl.BlockSpec((cycles, width, size, size), lambda j: (0, j, 0, 0)),
        ],
        out_specs=[constant(o.shape) for o in outs] + [part_spec, part_spec, ANY],
        out_shape=outs + [part, part, TOKEN],
        compiler_params=params(),
        cost_estimate=CHEAP,
        name="start",
    )(place, pivots, matrix)


class Chain:
    def __init__(self, token):
        self.token = token
        self.due = []

    def need(self, *arrays):
        self.due += arrays

    def run(self, kernel, name, operands, in_specs, out_shape, out_specs, **options):
        operands, in_specs = list(operands), list(in_specs)
        given, made = len(operands), len(out_shape)
        waits = [self.token, *self.due]
        self.due = []

        def body(*refs):
            kernel(*refs[:given], *refs[given + len(waits) : given + len(waits) + made], *refs[given + len(waits) + made + 1 :])

        *outs, self.token = pl.pallas_call(
            body,
            in_specs=in_specs + [ANY] * len(waits),
            out_specs=list(out_specs) + [ANY],
            out_shape=list(out_shape) + [TOKEN],
            compiler_params=params(),
            cost_estimate=CHEAP,
            name=name,
            **options,
        )(*operands, *waits)
        return outs

    def whole(self, kernel, name, place, operands, out_shape, **options):
        return self.run(
            kernel,
            name,
            (place, *operands),
            [SMEM] + [VMEM] * len(operands),
            out_shape,
            [VMEM] * len(out_shape),
            **options,
        )


def gather_rows(chain, matrix, onehot, first, count, width):
    cycles, _, size, _ = matrix.shape
    part = array(count, size, size)
    part_spec = pl.BlockSpec((width, size, size), lambda j: (j, 0, 0))
    return chain.run(
        gather_step,
        "gather_rows",
        (onehot, matrix),
        [
            constant(onehot.shape),
            pl.BlockSpec((cycles, width, size, size), lambda j: (0, j + first // width, 0, 0)),
        ],
        [part, part],
        [part_spec, part_spec],
        grid=(count // width,),
    )


def meet_kernel(place, mine_ref, theirs_ref, out_ref):
    out_ref[...] = mine_ref[...] + theirs_ref[...]


def merge_kernel(place, owner_ref, native_ref, received_ref, out_ref):
    own = jnp.logical_or(place[0] == 0, owner_ref[0] == place[0])
    for b in range(out_ref.shape[0]):
        out_ref[b] = jnp.where(own, native_ref[b], received_ref[b])


def finish_kernel(place, owner_ref, me_ref, native_ref, *refs):
    *received, mine_ref, send_ref = refs
    chips = len(received) + 1
    chip = place[0]
    owner = owner_ref[0]
    me = me_ref[0] != 0
    passed = jnp.logical_and(owner == chip, chip != 0)
    passed_mine = jnp.logical_and(passed, me)
    passed_other = jnp.logical_and(passed, jnp.logical_not(me))
    for at in range(chips):

        @pl.when(chip == at)
        def _(at=at):
            for b in range(native_ref.shape[0]):
                native = native_ref[b]
                left = received[at - 1][b] if at > 0 else native
                right = received[chips - 2 - at][b] if at < chips - 1 else native
                new = jnp.where(owner < chip, left, jnp.where(owner > chip, right, native))
                mine_ref[b] = jnp.where(passed_mine, left, new)
                send_ref[b] = jnp.where(passed_other, left, new)


def side_kernel(place, own_ref, down_ref, out_ref):
    out_ref[...] = jnp.where(place[2] < 2, own_ref[...], down_ref[...])


def pair_kernel(place, own_ref, down_ref, side_ref, *out_refs):
    near = jnp.where(place[2] < 2, own_ref[...], down_ref[...])
    even = place[2] % 2 == 0
    first = jnp.where(even, near, side_ref[...])
    second = jnp.where(even, side_ref[...], near)
    for i, out_ref in enumerate(out_refs):
        out_ref[0] = first[i]
        out_ref[1] = second[i]


def placement_kernel(place, lands_ref, put_ref, keep_ref):
    cycles, size, slots = put_ref.shape
    for cycle in range(cycles):
        at = iota((size, size), 0) + cycle * size
        halves = []
        for half in range(2):
            hit = jnp.where(lands_ref[half : half + 1] == at, 1.0, 0.0)
            put_ref[cycle, :, half * size : (half + 1) * size] = hit.astype(BF16)
            halves.append(hit)
        filled = jnp.sum(halves[0] + halves[1], axis=1, keepdims=True)
        keep_ref[cycle] = jnp.broadcast_to(1.0 - filled, (size, size)).astype(BF16)


def newton_inverse(diag, identity):
    third = 1.0 / 3.0
    approx = (2.0 * identity - diag * third) * third
    for _ in range(NEWTON - 1):
        approx = dot_full(approx, 2.0 * identity - dot_full(diag, approx))
    return approx


def split_dot(a, b):
    high = b.astype(BF16)
    rest = b - high.astype(F32)
    mid = rest.astype(BF16)
    low = (rest - mid.astype(F32)).astype(BF16)
    return dot(a, low) + dot(a, mid) + dot(a, high)


def whole_rows(place, me_ref, own_mine, own_other, x_mine, x_other):
    mine = jnp.where(me_ref[0] != 0, own_mine, x_mine)
    other = jnp.where(me_ref[1] != 0, own_other, x_other)
    first_core = place[1] == 0
    return jnp.where(first_core, mine, other), jnp.where(first_core, other, mine)


def old_rows(place, x_mine, x_other, top_mine, top_other):
    first_chip = place[0] == 0
    return jnp.concatenate(
        [
            jnp.where(first_chip, top_mine, x_mine),
            jnp.where(first_chip, top_other, x_other),
        ],
        axis=0,
    )


def panel_kernel(place, me_ref, xm_ref, xo_ref, top_ref, onehot_ref, put_ref, keep_ref, *rest):
    *pieces, side_ref, lower1_ref, corner_ref, raw0, raw1, sems = rest
    cycles, size, _ = raw0.shape
    row = 2 * place[0] + place[1]
    slots = STEPS * size

    def fetch(pairs):
        copies = []
        for target, sources in zip((raw0, raw1), pairs):
            at = 0
            for source in sources:
                count = source.shape[0]
                copies.append(
                    pltpu.make_async_copy(source, target.at[at : at + count], sems.at[len(copies)])
                )
                at += count
        for copy in copies:
            copy.start()
        for copy in copies:
            copy.wait()

    if len(pieces) == 2:
        fetch(((pieces[0],), (pieces[1],)))
    else:
        own, down, over = pieces[:2], pieces[2:4], pieces[4:]
        for col, pairs in enumerate(((own, over), (over, own), (down, over), (over, down))):

            @pl.when(place[2] == col)
            def _(pairs=pairs):
                fetch(pairs)

    new0, new1, old = [], [], []
    for b, raw in enumerate((raw0, raw1)):
        own = dot(onehot_ref[...], raw.reshape(cycles * size, size)[...]).astype(BF16)
        upper, below = whole_rows(place, me_ref, own[:size], own[size:], xm_ref[b], xo_ref[b])
        new0.append(upper)
        new1.append(below)
        old.append(old_rows(place, xm_ref[b], xo_ref[b], raw[0], top_ref[b]))
    identity = jnp.where(iota((size, size), 0) == iota((size, size), 1), 1.0, 0.0).astype(F32)
    inverse0 = newton_inverse(new0[0].astype(F32), identity)
    corner = split_dot(new1[0], inverse0).astype(BF16)
    corner_ref[...] = corner
    inverse1 = newton_inverse(
        (new1[1].astype(F32) - dot(corner, new0[1])).astype(BF16).astype(F32), identity
    )
    for cycle in range(cycles):
        put = put_ref[cycle]
        keep = keep_ref[cycle]
        left = (dot(put, old[0]) + (keep * raw0[cycle]).astype(F32)).astype(BF16)
        right = dot(put, old[1]) + (keep * raw1[cycle]).astype(F32)
        if cycle == 0:
            left = jnp.where(row == 0, new0[0], jnp.where(row == 1, new1[0], left))
            right = jnp.where(
                row == 0, new0[1].astype(F32), jnp.where(row == 1, new1[1].astype(F32), right)
            )
        lower = split_dot(left, inverse0)
        if cycle == 0:
            lower = jnp.where(row == 0, 0.0, lower)
        lower = lower.astype(BF16)
        side_ref[cycle, :, :slots] = put
        side_ref[cycle, :, slots:] = -lower
        right = (right - dot(lower, new0[1])).astype(BF16)
        lower = split_dot(right, inverse1)
        if cycle == 0:
            lower = jnp.where(row <= 1, 0.0, lower)
        lower1_ref[cycle] = lower.astype(BF16)


def factor_panels(chain, place, me, rows, tops, onehot, put, keep, pieces):
    cycles, size, _ = keep.shape
    operands = (place, me, *rows, tops, onehot, put, keep)
    return chain.run(
        panel_kernel,
        "factor_panels",
        (*operands, *pieces),
        [SMEM] + [VMEM] * (len(operands) - 1) + [ANY] * len(pieces),
        [
            array(cycles, size, (STEPS + 1) * size),
            array(cycles, size, size),
            array(size, size),
        ],
        [VMEM] * 3,
        scratch_shapes=[
            pltpu.VMEM((cycles, size, size), BF16),
            pltpu.VMEM((cycles, size, size), BF16),
            pltpu.SemaphoreType.DMA((len(pieces),)),
        ],
    )


def update_kernel(
    first, place, me_ref, block_ref, native_ref, own_ref, xm_ref, xo_ref, top_ref,
    side_ref, keep_ref, lower1_ref, corner_ref, *rest,
):
    out_ref = rest[-1]
    cycles, width, size, _ = block_ref.shape
    row = 2 * place[0] + place[1]
    slots = STEPS * size
    upper, below, old = [], [], []
    for b in range(width):
        u, n = whole_rows(place, me_ref, native_ref[b], own_ref[b], xm_ref[b], xo_ref[b])
        upper.append(u)
        below.append(n)
        old.append(old_rows(place, xm_ref[b], xo_ref[b], block_ref[0, b], top_ref[b]))
    join = lambda parts: parts[0] if width == 1 else jnp.concatenate(parts, 1)
    upper, below, old = join(upper), join(below), join(old)
    upper1 = (below.astype(F32) - dot(corner_ref[...], upper)).astype(BF16)
    both = jnp.concatenate([old, upper], 0)
    for cycle in range(cycles):
        keep = keep_ref[cycle]
        kept = join([block_ref[cycle, b] * keep for b in range(width)])
        block = (dot(side_ref[cycle], both) + kept.astype(F32)).astype(BF16)
        if cycle == 0:
            block = jnp.where(row == 0, upper, jnp.where(row == 1, upper1, block))
        block = (block.astype(F32) - dot(lower1_ref[cycle], upper1)).astype(BF16)
        for b in range(width):
            out_ref[cycle, b] = block[:, b * size : (b + 1) * size]
    if first == 0:

        @pl.when(jnp.logical_and(pl.program_id(0) == 0, place[2] == 0))
        def _():
            for cycle in range(cycles):
                block = -side_ref[cycle, :, slots:]
                if cycle == 0:
                    block = jnp.where(row == 0, upper[:, :size], block)
                out_ref[cycle, 0] = block

        @pl.when(jnp.logical_and(pl.program_id(0) == 0, place[2] == 1))
        def _():
            for cycle in range(cycles):
                block = lower1_ref[cycle]
                if cycle == 0:
                    block = jnp.where(
                        row == 0, upper[:, :size], jnp.where(row == 1, upper1[:, :size], block)
                    )
                out_ref[cycle, 0] = block


def update_columns(chain, place, me, matrix, rows, top, factors, first, count, width, result):
    cycles, blocks, size, _ = matrix.shape
    column = pl.BlockSpec((width, size, size), lambda j: (j, 0, 0))
    blocks_spec = pl.BlockSpec(
        (cycles, width, size, size), lambda j: (0, j + first // width, 0, 0)
    )
    operands = [place, me, matrix, *rows, top, *factors]
    in_specs = [SMEM, constant(me.shape), blocks_spec]
    in_specs += [column] * 4
    in_specs += [pl.BlockSpec((width, size, size), lambda j: (j + first // width, 0, 0))]
    in_specs += [constant(f.shape) for f in factors]
    aliases = {}
    if result is not None:
        aliases = {len(operands): 0}
        operands.append(result)
        in_specs.append(ANY)
    return chain.run(
        functools.partial(update_kernel, first),
        "update_columns",
        operands,
        in_specs,
        [array(*matrix.shape)],
        [blocks_spec],
        grid=(count // width,),
        input_output_aliases=aliases,
    )[0]


def split_blocks(blocks):
    width = 2 if blocks % 2 == 0 else 1
    base, extra = divmod(blocks // width - 1, 3)
    counts = [1] + [base + (1 if i < extra else 0) for i in range(3)]
    return width, [width * c for c in counts]


def body(matrix, pivots):
    rows = lax.axis_size("row")
    cols = lax.axis_size("col")
    chips = rows // 2
    row = lax.axis_index("row")
    col = lax.axis_index("col")
    cycles, size, blocks, _ = matrix.shape
    plain = matrix.transpose(0, 2, 1, 3)
    matrix = pltpu.with_memory_space_constraint(plain, pltpu.HBM)
    place = jnp.stack([row // 2, row % 2, col]).astype(I32)
    width, counts = split_blocks(blocks)
    starts = [sum(counts[:i]) for i in range(len(counts))]
    few_cols = cols == 4
    half = (cycles + 1) // 2

    swap = [(r, r ^ 1) for r in range(rows)]
    first_swap = [(0, 1), (1, 0)]
    down_pairs = [(0, 2), (1, 3)]
    side_pairs = [(0, 1), (1, 0), (2, 3), (3, 2)]

    def hop_pairs(h):
        pairs = []
        for a, b in ((h, h + 1), (chips - 1 - h, chips - 2 - h)):
            pairs += [(2 * a, 2 * b), (2 * a + 1, 2 * b + 1)]
        return pairs

    onehot, owner, me, lands, raw_a, raw_b, mine, other, token = start(
        place, pivots, matrix, counts[0], width, rows
    )
    chain = Chain(token)
    native, others, theirs, x_mine, x_send, x_other = {0: mine}, {0: other}, {}, {}, {}, {}
    hops = {i: [] for i in range(len(counts))}
    received = {i: [] for i in range(len(counts))}

    def swap_others(*chunks):
        own = [others[i] for i in chunks]
        own = own[0] if len(own) == 1 else jnp.concatenate(own, 0)
        theirs[chunks] = lax.ppermute(own, "row", swap)

    def gather(i, count):
        a, b = gather_rows(chain, matrix, onehot, starts[i], count, width)
        return a, b

    def meet(mine, theirs):
        return chain.whole(meet_kernel, "meet", place, (mine, theirs), [array(*mine.shape)])[0]

    def hop(i):
        h = len(hops[i])
        if h == 0:
            out = native[i]
        else:
            received[i].append(hops[i][h - 1])
            out = chain.whole(
                merge_kernel,
                "merge",
                place,
                (owner, native[i], received[i][h - 1]),
                [array(*native[i].shape)],
            )[0]
        hops[i].append(lax.ppermute(out, "row", hop_pairs(h)))

    def finish(i):
        while len(hops[i]) < chips - 1:
            hop(i)
        received[i].append(hops[i][-1])
        x_mine[i], x_send[i] = chain.whole(
            finish_kernel,
            "finish",
            place,
            (owner, me, native[i], *received[i]),
            [array(*native[i].shape)] * 2,
        )

    def exchange(i):
        x_other[i] = lax.ppermute(x_send[i], "row", swap)

    def side(own, down, axis_pairs=side_pairs):
        out = chain.whole(side_kernel, "side", place, (own, down), [array(*own.shape)])[0]
        return lax.ppermute(out, "col", side_pairs)

    def from_two(own):
        zero = jnp.zeros_like(own)
        return lax.psum(jnp.stack([jnp.where(col == b, own, zero) for b in range(2)]), "col")

    theirs0 = lax.ppermute(other, "row", swap)
    if few_cols:
        down_a = lax.ppermute(raw_a, "col", down_pairs)
        down_b = lax.ppermute(raw_b, "col", down_pairs)
    native[1], others[1] = gather(1, counts[1])
    theirs1 = lax.ppermute(others[1], "row", swap)
    native[0] = meet(mine, theirs0)
    hop(0)
    native[1] = meet(native[1], theirs1)
    hop(1)
    rest_mine, rest_other = gather(2, counts[2] + counts[3])
    rest_theirs = lax.ppermute(rest_other, "row", swap)
    hop(0)
    if few_cols:
        side_a = side(raw_a, down_a)
    rest = meet(rest_mine, rest_theirs)
    cut = counts[2]
    native[2], native[3] = rest[:cut], rest[cut:]
    others[2], others[3] = rest_other[:cut], rest_other[cut:]
    hop(2)
    if few_cols:
        side_b = side(raw_b, down_b)
    hop(0)
    hop(1)
    put, keep = chain.whole(
        placement_kernel,
        "placement",
        place,
        (lands,),
        [array(cycles, size, STEPS * size), array(cycles, size, size)],
    )
    if few_cols:
        chain.need(side_a)
    finish(0)
    lead = jnp.stack([x_mine[0][0], x_send[0][0]])
    if few_cols:
        down_lead = lax.ppermute(lead, "col", down_pairs)
    else:
        leads = from_two(lead)
        raws = from_two(jnp.concatenate([raw_a, raw_b], 0))
    hop(3)
    hop(2)
    if few_cols:
        chain.need(side_b)
    hop(1)
    exchange(0)
    if few_cols:
        side_lead = side(lead, down_lead)
        (firsts,) = chain.whole(
            pair_kernel, "pair", place, (raw_a, down_a, side_a), [array(2, size, size)]
        )
        pieces = [raw_a, raw_b, down_a, down_b, side_a, side_b]
    else:
        firsts = raws[:, 0]
        pieces = [raws[0], raws[1]]
    chain.need(x_other[0])
    tops = lax.ppermute(firsts, "row", first_swap)
    hop(3)
    if few_cols:
        panel_mine, panel_send = chain.whole(
            pair_kernel, "pair", place, (lead, down_lead, side_lead), [array(2, size, size)] * 2
        )
    else:
        panel_mine, panel_send = leads[:, 0], leads[:, 1]
    panel_other = lax.ppermute(panel_send, "row", swap)
    top = lax.ppermute(plain[0], "row", first_swap)
    hop(2)
    finish(1)
    exchange(1)
    side_rows, lower1, corner = factor_panels(
        chain, place, me, (panel_mine, panel_other), tops, onehot, put, keep, pieces
    )
    factors = (side_rows, keep, lower1, corner)

    def update(i, result):
        return update_columns(
            chain, place, me, matrix, (native[i], others[i], x_mine[i], x_other[i]), top,
            factors, starts[i], counts[i], width, result,
        )

    hop(3)
    result = update(0, None)
    result = update(1, result)
    finish(2)
    exchange(2)
    chain.need(x_other[2])
    finish(3)
    exchange(3)
    result = update(2, result)
    result = update(3, result)
    return result.transpose(0, 2, 1, 3)


def solution(mesh):
    return jax.shard_map(
        body,
        mesh=mesh,
        in_specs=(P(None, "row", None, "col"), P()),
        out_specs=P(None, "row", None, "col"),
        check_vma=False,
    )
```

```python
import functools

import jax
import jax.numpy as jnp
from jax import lax
from jax.experimental import pallas as pl
from jax.experimental.pallas import tpu as pltpu
from jax.sharding import PartitionSpec as P

STEPS = 2
NEWTON = 3
F32 = jnp.float32
BF16 = jnp.bfloat16
I32 = jnp.int32
VMEM_LIMIT = 24 * 1024 * 1024
CHEAP = pl.CostEstimate(flops=1024, bytes_accessed=1024, transcendentals=0)
ANY = pl.BlockSpec(memory_space=pl.ANY)
SMEM = pl.BlockSpec(memory_space=pltpu.SMEM)
VMEM = pl.BlockSpec(memory_space=pltpu.VMEM)


def dot(a, b):
    return jnp.dot(a, b, preferred_element_type=F32)


def dot_full(a, b):
    return jnp.dot(a, b, precision=lax.Precision.HIGHEST, preferred_element_type=F32)


def params():
    return pltpu.CompilerParams(vmem_limit_bytes=VMEM_LIMIT)


def iota(shape, dim):
    return lax.broadcasted_iota(I32, shape, dim)


def to_column(row):
    size = row.shape[1]
    diagonal = iota((size, size), 0) == iota((size, size), 1)
    return jnp.sum(jnp.where(diagonal, row.astype(F32), 0.0), axis=1, keepdims=True).astype(I32)


def to_row(column):
    size = column.shape[0]
    diagonal = iota((size, size), 0) == iota((size, size), 1)
    return jnp.sum(jnp.where(diagonal, column.astype(F32), 0.0), axis=0, keepdims=True).astype(I32)


def pick_sum(mask, value, axis):
    return jnp.sum(jnp.where(mask, value.astype(F32), 0.0), axis=axis, keepdims=True).astype(I32)


def start_kernel(
    rows, place, pivot_ref, matrix_ref, block_ref,
    onehot_ref, owner_ref, me_ref, lands_ref, raw_ref, mine_ref, other_ref, top_ref, token_ref, sem,
):
    copy = pltpu.make_async_copy(matrix_ref.at[0], top_ref, sem)
    copy.start()
    cycles, width, size, _ = block_ref.shape
    chip, core = place[0], place[1]
    row = 2 * chip + core

    @pl.when(pl.program_id(0) == 0)
    def _():
        square = (size, size)
        pivot0, pivot1 = pivot_ref[0:1], pivot_ref[1:2]
        column0 = to_column(pivot0)
        down, across = iota(square, 0), iota(square, 1)
        again = column0 == pivot1
        inner = column0 == across + size
        at = iota((1, size), 1)
        second = size + at + pick_sum(inner, down - across - size, 0)
        source1 = pivot1 + pick_sum(again, down - pivot1, 0)
        leaves0 = iota((size, 1), 0) + pick_sum(again, second - down, 1)
        device_of = lambda r: r // size % rows
        local_of = lambda r: r // (size * rows) * size + r % size

        def of_slots(source, leaves):
            device = device_of(source)
            owner = device // 2
            me = device == row
            come = jnp.where(jnp.logical_and(chip == 0, owner != 0), leaves, source)
            taken = jnp.where(device_of(come) == row, local_of(come), -1)
            return owner, me.astype(I32), taken

        first = of_slots(column0, leaves0)
        last = of_slots(to_column(source1), to_column(second))
        swapped = core == 1
        mine = [jnp.where(swapped, b, a) for a, b in zip(first, last)]
        other = [jnp.where(swapped, a, b) for a, b in zip(first, last)]
        for half, values in enumerate((mine, other)):
            owner_ref[half] = values[0]
            me_ref[half] = values[1]
            for cycle in range(cycles):
                hit = values[2] == across + cycle * size
                onehot_ref[half * size : (half + 1) * size, cycle * size : (cycle + 1) * size] = (
                    jnp.where(hit, 1.0, 0.0).astype(BF16)
                )

        slots = STEPS * size
        lands = []
        for source in (pivot0, source1):
            outside = jnp.logical_and(device_of(source) == row, source >= slots)
            lands.append(jnp.where(outside, local_of(source), -1))
        by_top = []
        leaving = (leaves0, to_column(second))
        landing = [to_column(v) for v in lands]
        for half in range(2):
            total = jnp.full((1, size), -1, I32)
            for leave, land in zip(leaving, landing):
                total += pick_sum(leave == across + half * size, land + 1, 0)
            by_top.append(total)
        lands = [jnp.where(chip == 0, a, b) for a, b in zip(by_top, lands)]
        lands_ref[0:1] = jnp.where(swapped, lands[1], lands[0])
        lands_ref[1:2] = jnp.where(swapped, lands[0], lands[1])
        raw_ref[...] = block_ref[:, 0]

    gather_step(onehot_ref, block_ref, mine_ref, other_ref)
    copy.wait()


def gather_step(onehot_ref, block_ref, mine_ref, other_ref):
    cycles, width, size, _ = block_ref.shape
    columns = [
        jnp.concatenate([block_ref[cycle, b] for cycle in range(cycles)], 0) for b in range(width)
    ]
    columns = columns[0] if width == 1 else jnp.concatenate(columns, 1)
    total = dot(onehot_ref[...], columns).astype(BF16)
    for b in range(width):
        mine_ref[b] = total[:size, b * size : (b + 1) * size]
        other_ref[b] = total[size:, b * size : (b + 1) * size]


def constant(shape):
    return pl.BlockSpec(
        shape, lambda *j, n=len(shape): (0,) * n, pipeline_mode=pl.Buffered(1)
    )


def array(*shape, dtype=BF16):
    return jax.ShapeDtypeStruct(shape, dtype)


TOKEN = array(8, 128, dtype=F32)


def start(place, pivots, matrix, width, rows):
    cycles, blocks, size, _ = matrix.shape
    slots = STEPS * size
    part = array(width, size, size)
    outs = [
        array(slots, cycles * size),
        array(2, size, 1, dtype=I32),
        array(2, size, 1, dtype=I32),
        array(2, size, dtype=I32),
        array(cycles, size, size),
        part,
        part,
    ]
    return pl.pallas_call(
        functools.partial(start_kernel, rows),
        grid=(1,),
        in_specs=[
            SMEM,
            constant(pivots.shape),
            ANY,
            pl.BlockSpec((cycles, width, size, size), lambda j: (0, 0, 0, 0)),
        ],
        out_specs=[constant(o.shape) for o in outs] + [ANY, ANY],
        out_shape=outs + [array(blocks, size, size), TOKEN],
        scratch_shapes=[pltpu.SemaphoreType.DMA],
        compiler_params=params(),
        cost_estimate=CHEAP,
        name="start",
    )(place, pivots, matrix, matrix)


class Chain:
    def __init__(self, token):
        self.token = token
        self.due = []
        self.held = []

    def hold(self, *arrays):
        self.held = list(arrays)

    def need(self, *arrays):
        self.due += arrays

    def run(self, kernel, name, operands, in_specs, out_shape, out_specs, **options):
        operands, in_specs = list(operands), list(in_specs)
        given, made = len(operands), len(out_shape)
        held, waits = self.held, [self.token, *self.due]
        self.due, self.held = [], []
        aliases = dict(options.pop("input_output_aliases", {}))
        for i in range(len(held)):
            aliases[given + len(waits) + i] = made + 1 + i
        passed = len(held)

        def inner(*refs):
            outs = given + len(waits) + passed
            kernel(*refs[:given], *refs[outs : outs + made], *refs[outs + made + 1 + passed :])

        outs = pl.pallas_call(
            inner,
            in_specs=in_specs + [ANY] * (len(waits) + passed),
            out_specs=list(out_specs) + [ANY] * (1 + passed),
            out_shape=list(out_shape) + [TOKEN] + [array(*a.shape) for a in held],
            input_output_aliases=aliases,
            compiler_params=params(),
            cost_estimate=CHEAP,
            name=name,
            **options,
        )(*operands, *waits, *held)
        self.token, self.passed = outs[made], outs[made + 1 :]
        return outs[:made]

    def whole(self, kernel, name, place, operands, out_shape, **options):
        return self.run(
            kernel,
            name,
            (place, *operands),
            [SMEM] + [VMEM] * len(operands),
            out_shape,
            [VMEM] * len(out_shape),
            **options,
        )


def gather_rows(chain, matrix, onehot, first, count, width):
    cycles, _, size, _ = matrix.shape
    part = array(count, size, size)
    part_spec = pl.BlockSpec((width, size, size), lambda j: (j, 0, 0))
    return chain.run(
        gather_step,
        "gather_rows",
        (onehot, matrix),
        [
            VMEM,
            pl.BlockSpec((cycles, width, size, size), lambda j: (0, j + first // width, 0, 0)),
        ],
        [part, part],
        [part_spec, part_spec],
        grid=(count // width,),
    )


def meet_kernel(place, mine_ref, theirs_ref, *out_refs):
    at = 0
    for out_ref in out_refs:
        count = out_ref.shape[0]
        out_ref[...] = mine_ref[at : at + count] + theirs_ref[at : at + count]
        at += count


def meet_more_kernel(place, mine_ref, theirs_ref, extra_ref, out_ref):
    count = mine_ref.shape[0]
    out_ref[:count] = mine_ref[...] + theirs_ref[...]
    out_ref[count:] = extra_ref[...]


def lead_kernel(place, mine_ref, other_ref, out_ref):
    out_ref[0] = mine_ref[0]
    out_ref[1] = other_ref[0]


def merge_kernel(place, owner_ref, native_ref, received_ref, out_ref):
    own = jnp.logical_or(place[0] == 0, owner_ref[0] == place[0])
    for b in range(out_ref.shape[0]):
        out_ref[b] = jnp.where(own, native_ref[b], received_ref[b])


def merge_or_send_kernel(place, owner_ref, native_ref, received_ref, fresh_ref, out_ref, *, chips):
    own = jnp.logical_or(place[0] == 0, owner_ref[0] == place[0])
    end = jnp.logical_or(place[0] == 0, place[0] == chips - 1)
    for b in range(out_ref.shape[0]):
        merged = jnp.where(own, native_ref[b], received_ref[b])
        out_ref[b] = jnp.where(end, fresh_ref[b], merged)


def finish_kernel(place, owner_ref, me_ref, native_ref, *refs):
    *received, mine_ref, send_ref = refs
    chips = len(received) + 1
    chip = place[0]
    owner = owner_ref[0]
    me = me_ref[0] != 0
    passed = jnp.logical_and(owner == chip, chip != 0)
    passed_mine = jnp.logical_and(passed, me)
    passed_other = jnp.logical_and(passed, jnp.logical_not(me))
    for at in range(chips):

        @pl.when(chip == at)
        def _(at=at):
            for b in range(native_ref.shape[0]):
                native = native_ref[b]
                left = received[at - 1][b] if at > 0 else native
                right = received[chips - 2 - at][b] if at < chips - 1 else native
                new = jnp.where(owner < chip, left, jnp.where(owner > chip, right, native))
                mine_ref[b] = jnp.where(passed_mine, left, new)
                send_ref[b] = jnp.where(passed_other, left, new)


def side_kernel(place, own_ref, down_ref, out_ref):
    out_ref[...] = jnp.where(place[2] < 2, own_ref[...], down_ref[...])


def pair_kernel(place, own_ref, down_ref, side_ref, *out_refs):
    near = jnp.where(place[2] < 2, own_ref[...], down_ref[...])
    even = place[2] % 2 == 0
    first = jnp.where(even, near, side_ref[...])
    second = jnp.where(even, side_ref[...], near)
    for i, out_ref in enumerate(out_refs):
        out_ref[0] = first[i]
        out_ref[1] = second[i]


def placement_kernel(place, lands_ref, put_ref, keep_ref):
    cycles, size, slots = put_ref.shape
    for cycle in range(cycles):
        at = iota((size, size), 0) + cycle * size
        halves = []
        for half in range(2):
            hit = jnp.where(lands_ref[half : half + 1] == at, 1.0, 0.0)
            put_ref[cycle, :, half * size : (half + 1) * size] = hit.astype(BF16)
            halves.append(hit)
        filled = jnp.sum(halves[0] + halves[1], axis=1, keepdims=True)
        keep_ref[cycle] = jnp.broadcast_to(1.0 - filled, (size, size)).astype(BF16)


def placement(chain, place, lands, cycles):
    size = lands.shape[1]
    return chain.whole(
        placement_kernel,
        "placement",
        place,
        (lands,),
        [array(cycles, size, STEPS * size), array(cycles, size, size)],
    )


def three_parts(a):
    high = a.astype(BF16)
    rest = a - high.astype(F32)
    mid = rest.astype(BF16)
    low = (rest - mid.astype(F32)).astype(BF16)
    return jnp.concatenate([low, mid, high], 1)


def sum_parts(a):
    size = a.shape[1] // 3
    return (a[:, :size] + a[:, size : 2 * size]) + a[:, 2 * size :]


def newton_inverse(diag, identity):
    third = 1.0 / 3.0
    approx = (2.0 * identity - diag.astype(F32) * third) * third
    for _ in range(NEWTON - 1):
        product = sum_parts(dot(diag, three_parts(approx)))
        approx = dot_full(approx, 2.0 * identity - product)
    return approx


def whole_rows(place, me_ref, own_mine, own_other, x_mine, x_other):
    mine = jnp.where(me_ref[0] != 0, own_mine, x_mine)
    other = jnp.where(me_ref[1] != 0, own_other, x_other)
    first_core = place[1] == 0
    return jnp.where(first_core, mine, other), jnp.where(first_core, other, mine)


def old_rows(place, x_mine, x_other, top_mine, top_other):
    first_chip = place[0] == 0
    return jnp.concatenate(
        [
            jnp.where(first_chip, top_mine, x_mine),
            jnp.where(first_chip, top_other, x_other),
        ],
        axis=0,
    )


def panel_kernel(place, me_ref, xm_ref, xo_ref, top_ref, onehot_ref, put_ref, keep_ref, *rest):
    *pieces, side_ref, lower1_ref, corner_ref, raw0, raw1, sems = rest
    cycles, size, _ = raw0.shape
    row = 2 * place[0] + place[1]
    slots = STEPS * size

    def fetch(pairs):
        copies = []
        for target, sources in zip((raw0, raw1), pairs):
            at = 0
            for source in sources:
                count = source.shape[0]
                copies.append(
                    pltpu.make_async_copy(source, target.at[at : at + count], sems.at[len(copies)])
                )
                at += count
        for copy in copies:
            copy.start()
        for copy in copies:
            copy.wait()

    if len(pieces) == 2:
        fetch(((pieces[0],), (pieces[1],)))
    else:
        own, down, over = ((piece,) for piece in pieces)
        for col, pairs in enumerate(((own, over), (over, own), (down, over), (over, down))):

            @pl.when(place[2] == col)
            def _(pairs=pairs):
                fetch(pairs)

    flat = [raw.reshape(cycles * size, size)[...] for raw in (raw0, raw1)]
    own = dot(onehot_ref[...], jnp.concatenate(flat, 1)).astype(BF16)
    new0, new1, old = [], [], []
    for b, raw in enumerate((raw0, raw1)):
        mine, other = own[:size, b * size : (b + 1) * size], own[size:, b * size : (b + 1) * size]
        upper, below = whole_rows(place, me_ref, mine, other, xm_ref[b], xo_ref[b])
        new0.append(upper)
        new1.append(below)
        old.append(old_rows(place, xm_ref[b], xo_ref[b], raw[0], top_ref[b]))
    old = jnp.concatenate(old, 1)
    identity = jnp.where(iota((size, size), 0) == iota((size, size), 1), 1.0, 0.0).astype(F32)
    inverse0 = three_parts(newton_inverse(new0[0], identity))
    corner = sum_parts(dot(new1[0], inverse0)).astype(BF16)
    corner_ref[...] = corner
    inverse1 = three_parts(
        newton_inverse((new1[1].astype(F32) - dot(corner, new0[1])).astype(BF16), identity)
    )
    for cycle in range(cycles):
        put = put_ref[cycle]
        keep = keep_ref[cycle]
        both = dot(put, old)
        left = (both[:, :size] + (keep * raw0[cycle]).astype(F32)).astype(BF16)
        right = both[:, size:] + (keep * raw1[cycle]).astype(F32)
        if cycle == 0:
            left = jnp.where(row == 0, new0[0], jnp.where(row == 1, new1[0], left))
            right = jnp.where(
                row == 0, new0[1].astype(F32), jnp.where(row == 1, new1[1].astype(F32), right)
            )
        lower = sum_parts(dot(left, inverse0))
        if cycle == 0:
            lower = jnp.where(row == 0, 0.0, lower)
        lower = lower.astype(BF16)
        side_ref[cycle, :, :slots] = put
        side_ref[cycle, :, slots:] = -lower
        right = (right - dot(lower, new0[1])).astype(BF16)
        lower = sum_parts(dot(right, inverse1))
        if cycle == 0:
            lower = jnp.where(row <= 1, 0.0, lower)
        lower1_ref[cycle] = lower.astype(BF16)


def factor_panels(chain, place, me, rows, tops, onehot, put, keep, pieces):
    cycles, size, _ = keep.shape
    return chain.run(
        panel_kernel,
        "factor_panels",
        (place, me, *rows, tops, onehot, put, keep, *pieces),
        [SMEM] + [VMEM] * 7 + [ANY] * len(pieces),
        [
            array(cycles, size, (STEPS + 1) * size),
            array(cycles, size, size),
            array(size, size),
        ],
        [VMEM] * 3,
        scratch_shapes=[
            pltpu.VMEM((cycles, size, size), BF16),
            pltpu.VMEM((cycles, size, size), BF16),
            pltpu.SemaphoreType.DMA((4,)),
        ],
    )


def update_kernel(first, counts, place, me_ref, block_ref, top_ref, *rest):
    sets = [rest[4 * i : 4 * i + 4] for i in range(len(counts))]
    side_ref, keep_ref, lower1_ref, corner_ref = rest[4 * len(counts) : 4 * len(counts) + 4]
    out_ref, both_ref, below_ref = rest[-3:]
    cycles, width, size, _ = block_ref.shape
    at = pl.program_id(0) * width
    row = 2 * place[0] + place[1]
    slots = STEPS * size
    start = 0
    for (native_ref, own_ref, xm_ref, xo_ref), count in zip(sets, counts):

        def prepare(start=start, native_ref=native_ref, own_ref=own_ref, xm_ref=xm_ref, xo_ref=xo_ref):
            for b in range(width):
                i = at + (b - start)
                xm, xo = xm_ref[i], xo_ref[i]
                upper, below = whole_rows(place, me_ref, native_ref[i], own_ref[i], xm, xo)
                old = old_rows(place, xm, xo, block_ref[0, b], top_ref[b])
                part = slice(b * size, (b + 1) * size)
                both_ref[:slots, part] = old
                both_ref[slots:, part] = upper
                below_ref[:, part] = below

        if len(counts) == 1:
            prepare()
        else:
            pl.when(jnp.logical_and(at >= start, at < start + count))(prepare)
        start += count
    join = lambda parts: parts[0] if width == 1 else jnp.concatenate(parts, 1)
    both = both_ref[...]
    upper = both[slots:]
    upper1 = (below_ref[...].astype(F32) - dot(corner_ref[...], upper)).astype(BF16)
    for cycle in range(cycles):
        keep = keep_ref[cycle]
        kept = join([block_ref[cycle, b] * keep for b in range(width)])
        block = (dot(side_ref[cycle], both) + kept.astype(F32)).astype(BF16)
        if cycle == 0:
            block = jnp.where(row == 0, upper, jnp.where(row == 1, upper1, block))
        block = (block.astype(F32) - dot(lower1_ref[cycle], upper1)).astype(BF16)
        for b in range(width):
            out_ref[cycle, b] = block[:, b * size : (b + 1) * size]
    if first == 0:

        @pl.when(jnp.logical_and(pl.program_id(0) == 0, place[2] == 0))
        def _():
            for cycle in range(cycles):
                block = -side_ref[cycle, :, slots:]
                if cycle == 0:
                    block = jnp.where(row == 0, upper[:, :size], block)
                out_ref[cycle, 0] = block

        @pl.when(jnp.logical_and(pl.program_id(0) == 0, place[2] == 1))
        def _():
            for cycle in range(cycles):
                block = lower1_ref[cycle]
                if cycle == 0:
                    block = jnp.where(
                        row == 0, upper[:, :size], jnp.where(row == 1, upper1[:, :size], block)
                    )
                out_ref[cycle, 0] = block


def update_columns(chain, place, me, matrix, sets, top, factors, first, width, result):
    cycles, blocks, size, _ = matrix.shape
    counts = [s[0].shape[0] for s in sets]
    rows = [r for s in sets for r in s]
    at = lambda j: j + first // width
    blocks_spec = pl.BlockSpec((cycles, width, size, size), lambda j: (0, at(j), 0, 0))
    top_spec = pl.BlockSpec((width, size, size), lambda j: (at(j), 0, 0))
    operands = [place, me, matrix, top, *rows, *factors]
    in_specs = [SMEM, VMEM, blocks_spec, top_spec]
    in_specs += [VMEM] * (len(rows) + len(factors))
    aliases = {}
    if result is not None:
        aliases = {len(operands): 0}
        operands.append(result)
        in_specs.append(ANY)
    return chain.run(
        functools.partial(update_kernel, first, counts),
        "update_columns",
        operands,
        in_specs,
        [array(*matrix.shape)],
        [blocks_spec],
        grid=(sum(counts) // width,),
        scratch_shapes=[
            pltpu.VMEM(((STEPS + 1) * size, width * size), BF16),
            pltpu.VMEM((size, width * size), BF16),
        ],
        input_output_aliases=aliases,
    )[0]


def split_blocks(blocks):
    width = 2 if blocks % 2 == 0 else 1
    base, extra = divmod(blocks // width - 1, 3)
    counts = [width] + [width * (base + (1 if i < extra else 0)) for i in range(3)]
    return width, [(sum(counts[:i]), c) for i, c in enumerate(counts)]


def body(matrix, pivots):
    rows = lax.axis_size("row")
    cols = lax.axis_size("col")
    chips = rows // 2
    row = lax.axis_index("row")
    col = lax.axis_index("col")
    cycles, size, blocks, _ = matrix.shape
    plain = matrix.transpose(0, 2, 1, 3)
    matrix = pltpu.with_memory_space_constraint(plain, pltpu.HBM)
    place = jnp.stack([row // 2, row % 2, col]).astype(I32)
    width, chunks = split_blocks(blocks)
    count = len(chunks)
    few_cols = cols == 4

    swap = [(r, r ^ 1) for r in range(rows)]
    first_swap = [(0, 1), (1, 0)]
    down_pairs = [(0, 2), (1, 3)]
    side_pairs = [(0, 1), (1, 0), (2, 3), (3, 2)]

    def hop_pairs(h):
        pairs = []
        for a, b in ((h, h + 1), (chips - 1 - h, chips - 2 - h)):
            pairs += [(2 * a, 2 * b), (2 * a + 1, 2 * b + 1)]
        return pairs

    onehot, owner, me, lands, raw, mine, other, top, token = start(
        place, pivots, matrix, width, rows
    )
    chain = Chain(token)
    native, others, x_mine, x_send, x_other = {}, {}, {}, {}, {}
    hops = {i: [] for i in range(count)}

    def exchange(own):
        return lax.ppermute(own, "row", swap)

    def gather(i, blocks):
        return gather_rows(chain, matrix, onehot, chunks[i][0], blocks, width)

    def meet(mine, theirs, *counts):
        return chain.whole(
            meet_kernel, "meet", place, (mine, theirs), [array(c, size, size) for c in counts]
        )

    def hop(i):
        h = len(hops[i])
        out = native[i]
        if h:
            (out,) = chain.whole(
                merge_kernel,
                "merge",
                place,
                (owner, native[i], hops[i][-1]),
                [array(*native[i].shape)],
            )
        hops[i].append(lax.ppermute(out, "row", hop_pairs(h)))

    def finish(i):
        while len(hops[i]) < chips - 1:
            hop(i)
        x_mine[i], x_send[i] = chain.whole(
            finish_kernel,
            "finish",
            place,
            (owner, me, native[i], *hops[i]),
            [array(*native[i].shape)] * 2,
        )
        x_other[i] = exchange(x_send[i])

    def side(own, down):
        (out,) = chain.whole(side_kernel, "side", place, (own, down), [array(*own.shape)])
        return lax.ppermute(out, "col", side_pairs)

    def down(own):
        return lax.ppermute(own, "col", down_pairs)

    def pair(own, down, side, made):
        return chain.whole(
            pair_kernel, "pair", place, (own, down, side), [array(2, size, size)] * made
        )

    def from_two(own):
        zero = jnp.zeros_like(own)
        return lax.psum(jnp.stack([jnp.where(col == b, own, zero) for b in range(2)]), "col")

    def hop_both(i, j):
        if chips != 4 or native[i].shape != native[j].shape:
            hop(i)
            hop(j)
            return
        (out,) = chain.whole(
            functools.partial(merge_or_send_kernel, chips=chips),
            "merge",
            place,
            (owner, native[i], hops[i][-1], native[j]),
            [array(*native[i].shape)],
        )
        arrived = lax.ppermute(out, "row", hop_pairs(0) + hop_pairs(2))
        hops[i].append(arrived)
        hops[j].append(arrived)

    native[0], others[0] = mine, other
    theirs0 = exchange(other)
    if few_cols:
        down_raw = down(raw)
    sizes = [c for _, c in chunks]
    cut = sizes[1]
    some_mine, some_other = gather(1, sizes[1] + sizes[2])
    chain.hold(some_other)
    (native[0],) = meet(mine, theirs0, width)
    (some_other,) = chain.passed
    hop(0)
    some_theirs = exchange(some_other)
    others[1], others[2] = some_other[:cut], some_other[cut:]
    mine3, others[3] = gather(3, sizes[3])
    chain.hold(others[3])
    native[1], native[2] = meet(some_mine, some_theirs, sizes[1], sizes[2])
    (others[3],) = chain.passed
    hop(1)
    theirs3 = exchange(others[3])
    chain.hold(native[2])
    hop(0)
    (native[2],) = chain.passed
    hop(2)
    put, keep = placement(chain, place, lands, cycles)
    if few_cols:
        side_raw = side(raw, down_raw)
    hop(0)
    (native[3],) = meet(mine3, theirs3, sizes[3])
    hop(1)
    finish(0)
    (lead,) = chain.whole(
        lead_kernel, "lead", place, (x_mine[0], x_other[0]), [array(2, size, size)]
    )
    if few_cols:
        down_lead = down(lead)
    else:
        leads = from_two(lead)
    hop(2)
    hop_both(1, 3)
    if few_cols:
        side_lead = side(lead, down_lead)
    if few_cols:
        (firsts,) = pair(raw, down_raw, side_raw, 1)
    else:
        raws = from_two(raw)
        firsts = raws[:, 0]
    tops = lax.ppermute(firsts, "row", first_swap)
    if few_cols:
        panel_mine, panel_other = pair(lead, down_lead, side_lead, 2)
        pieces = [raw, down_raw, side_raw]
    else:
        panel_mine, panel_other = leads[:, 0], leads[:, 1]
        pieces = [raws[0], raws[1]]
    hop(2)
    hop(3)
    finish(1)
    side_rows, lower1, corner = factor_panels(
        chain, place, me, (panel_mine, panel_other), tops, onehot, put, keep, pieces
    )
    factors = (side_rows, keep, lower1, corner)

    def update(which, result):
        sets = [(native[i], others[i], x_mine[i], x_other[i]) for i in which]
        return update_columns(
            chain, place, me, matrix, sets, top, factors, chunks[which[0]][0], width, result
        )

    finish(2)
    chain.hold(top)
    hop(3)
    (top,) = chain.passed
    top = lax.ppermute(top, "row", first_swap)
    result = update((0, 1, 2), None)
    finish(3)
    result = update((3,), result)
    return result.transpose(0, 2, 1, 3)


def solution(mesh):
    return jax.shard_map(
        body,
        mesh=mesh,
        in_specs=(P(None, "row", None, "col"), P()),
        out_specs=P(None, "row", None, "col"),
        check_vma=False,
    )
```

```python
import functools

import jax
import jax.numpy as jnp
from jax import lax
from jax.experimental import pallas as pl
from jax.experimental.pallas import tpu as pltpu
from jax.sharding import PartitionSpec as P

STEPS = 2
NEWTON = 3
F32 = jnp.float32
BF16 = jnp.bfloat16
I32 = jnp.int32
VMEM_LIMIT = 24 * 1024 * 1024
CHEAP = pl.CostEstimate(flops=1024, bytes_accessed=1024, transcendentals=0)
ANY = pl.BlockSpec(memory_space=pl.ANY)
SMEM = pl.BlockSpec(memory_space=pltpu.SMEM)
VMEM = pl.BlockSpec(memory_space=pltpu.VMEM)


def dot(a, b):
    return jnp.dot(a, b, preferred_element_type=F32)


def dot_full(a, b):
    return jnp.dot(a, b, precision=lax.Precision.HIGHEST, preferred_element_type=F32)


def params():
    return pltpu.CompilerParams(vmem_limit_bytes=VMEM_LIMIT)


def iota(shape, dim):
    return lax.broadcasted_iota(I32, shape, dim)


def to_column(row):
    size = row.shape[1]
    diagonal = iota((size, size), 0) == iota((size, size), 1)
    return jnp.sum(jnp.where(diagonal, row.astype(F32), 0.0), axis=1, keepdims=True).astype(I32)


def to_row(column):
    size = column.shape[0]
    diagonal = iota((size, size), 0) == iota((size, size), 1)
    return jnp.sum(jnp.where(diagonal, column.astype(F32), 0.0), axis=0, keepdims=True).astype(I32)


def pick_sum(mask, value, axis):
    return jnp.sum(jnp.where(mask, value.astype(F32), 0.0), axis=axis, keepdims=True).astype(I32)


def start_kernel(
    rows, place, pivot_ref, matrix_ref, block_ref,
    onehot_ref, owner_ref, me_ref, lands_ref, raw_ref, mine_ref, other_ref, top_ref, token_ref, sem,
):
    copy = pltpu.make_async_copy(matrix_ref.at[0], top_ref, sem)
    copy.start()
    cycles, width, size, _ = block_ref.shape
    chip, core = place[0], place[1]
    row = 2 * chip + core

    @pl.when(pl.program_id(0) == 0)
    def _():
        square = (size, size)
        pivot0, pivot1 = pivot_ref[0:1], pivot_ref[1:2]
        column0 = to_column(pivot0)
        down, across = iota(square, 0), iota(square, 1)
        again = column0 == pivot1
        inner = column0 == across + size
        at = iota((1, size), 1)
        second = size + at + pick_sum(inner, down - across - size, 0)
        source1 = pivot1 + pick_sum(again, down - pivot1, 0)
        leaves0 = iota((size, 1), 0) + pick_sum(again, second - down, 1)
        device_of = lambda r: r // size % rows
        local_of = lambda r: r // (size * rows) * size + r % size

        def of_slots(source, leaves):
            device = device_of(source)
            owner = device // 2
            me = device == row
            come = jnp.where(jnp.logical_and(chip == 0, owner != 0), leaves, source)
            taken = jnp.where(device_of(come) == row, local_of(come), -1)
            return owner, me.astype(I32), taken

        first = of_slots(column0, leaves0)
        last = of_slots(to_column(source1), to_column(second))
        swapped = core == 1
        mine = [jnp.where(swapped, b, a) for a, b in zip(first, last)]
        other = [jnp.where(swapped, a, b) for a, b in zip(first, last)]
        for half, values in enumerate((mine, other)):
            owner_ref[half] = values[0]
            me_ref[half] = values[1]
            for cycle in range(cycles):
                hit = values[2] == across + cycle * size
                onehot_ref[half * size : (half + 1) * size, cycle * size : (cycle + 1) * size] = (
                    jnp.where(hit, 1.0, 0.0).astype(BF16)
                )

        slots = STEPS * size
        lands = []
        for source in (pivot0, source1):
            outside = jnp.logical_and(device_of(source) == row, source >= slots)
            lands.append(jnp.where(outside, local_of(source), -1))
        by_top = []
        leaving = (leaves0, to_column(second))
        landing = [to_column(v) for v in lands]
        for half in range(2):
            total = jnp.full((1, size), -1, I32)
            for leave, land in zip(leaving, landing):
                total += pick_sum(leave == across + half * size, land + 1, 0)
            by_top.append(total)
        lands = [jnp.where(chip == 0, a, b) for a, b in zip(by_top, lands)]
        lands_ref[0:1] = jnp.where(swapped, lands[1], lands[0])
        lands_ref[1:2] = jnp.where(swapped, lands[0], lands[1])
        raw_ref[...] = block_ref[:, 0]

    gather_step(onehot_ref, block_ref, mine_ref, other_ref)
    copy.wait()


def gather_step(onehot_ref, block_ref, mine_ref, other_ref):
    cycles, width, size, _ = block_ref.shape
    columns = [
        jnp.concatenate([block_ref[cycle, b] for cycle in range(cycles)], 0) for b in range(width)
    ]
    columns = columns[0] if width == 1 else jnp.concatenate(columns, 1)
    total = dot(onehot_ref[...], columns).astype(BF16)
    for b in range(width):
        mine_ref[b] = total[:size, b * size : (b + 1) * size]
        other_ref[b] = total[size:, b * size : (b + 1) * size]


def constant(shape):
    return pl.BlockSpec(
        shape, lambda *j, n=len(shape): (0,) * n, pipeline_mode=pl.Buffered(1)
    )


def array(*shape, dtype=BF16):
    return jax.ShapeDtypeStruct(shape, dtype)


TOKEN = array(8, 128, dtype=F32)


def start(place, pivots, matrix, width, rows):
    cycles, blocks, size, _ = matrix.shape
    slots = STEPS * size
    part = array(width, size, size)
    outs = [
        array(slots, cycles * size),
        array(2, size, 1, dtype=I32),
        array(2, size, 1, dtype=I32),
        array(2, size, dtype=I32),
        array(cycles, size, size),
        part,
        part,
    ]
    return pl.pallas_call(
        functools.partial(start_kernel, rows),
        grid=(1,),
        in_specs=[
            SMEM,
            constant(pivots.shape),
            ANY,
            pl.BlockSpec((cycles, width, size, size), lambda j: (0, 0, 0, 0)),
        ],
        out_specs=[constant(o.shape) for o in outs] + [ANY, ANY],
        out_shape=outs + [array(blocks, size, size), TOKEN],
        scratch_shapes=[pltpu.SemaphoreType.DMA],
        compiler_params=params(),
        cost_estimate=CHEAP,
        name="start",
    )(place, pivots, matrix, matrix)


class Chain:
    def __init__(self, token):
        self.token = token
        self.due = []
        self.held = []

    def hold(self, *arrays):
        self.held = list(arrays)

    def need(self, *arrays):
        self.due += arrays

    def run(self, kernel, name, operands, in_specs, out_shape, out_specs, **options):
        operands, in_specs = list(operands), list(in_specs)
        given, made = len(operands), len(out_shape)
        held, waits = self.held, [self.token, *self.due]
        self.due, self.held = [], []
        aliases = dict(options.pop("input_output_aliases", {}))
        for i in range(len(held)):
            aliases[given + len(waits) + i] = made + 1 + i
        passed = len(held)

        def inner(*refs):
            outs = given + len(waits) + passed
            kernel(*refs[:given], *refs[outs : outs + made], *refs[outs + made + 1 + passed :])

        outs = pl.pallas_call(
            inner,
            in_specs=in_specs + [ANY] * (len(waits) + passed),
            out_specs=list(out_specs) + [ANY] * (1 + passed),
            out_shape=list(out_shape) + [TOKEN] + [array(*a.shape) for a in held],
            input_output_aliases=aliases,
            compiler_params=params(),
            cost_estimate=CHEAP,
            name=name,
            **options,
        )(*operands, *waits, *held)
        self.token, self.passed = outs[made], outs[made + 1 :]
        return outs[:made]

    def whole(self, kernel, name, place, operands, out_shape, **options):
        return self.run(
            kernel,
            name,
            (place, *operands),
            [SMEM] + [VMEM] * len(operands),
            out_shape,
            [VMEM] * len(out_shape),
            **options,
        )


    def together(self, place, parts):
        def kernel(place_ref, *refs):
            at, made = 0, sum(len(part[1]) for part in parts)
            for part, operands, shapes in parts:
                part(place_ref, *refs[at : at + len(operands)], *refs[made : made + len(shapes)])
                at += len(operands)
                made += len(shapes)

        name = "_".join(getattr(part[0], "func", part[0]).__name__[:-7] for part in parts)
        outs = self.whole(
            kernel,
            name,
            place,
            [operand for part in parts for operand in part[1]],
            [shape for part in parts for shape in part[2]],
        )
        split, at = [], 0
        for part in parts:
            split.append(outs[at : at + len(part[2])])
            at += len(part[2])
        return split


def gather_rows(chain, matrix, onehot, first, count, width):
    cycles, _, size, _ = matrix.shape
    part = array(count, size, size)
    part_spec = pl.BlockSpec((width, size, size), lambda j: (j, 0, 0))
    return chain.run(
        gather_step,
        "gather_rows",
        (onehot, matrix),
        [
            VMEM,
            pl.BlockSpec((cycles, width, size, size), lambda j: (0, j + first // width, 0, 0)),
        ],
        [part, part],
        [part_spec, part_spec],
        grid=(count // width,),
    )


def meet_kernel(place, mine_ref, theirs_ref, *out_refs):
    at = 0
    for out_ref in out_refs:
        count = out_ref.shape[0]
        out_ref[...] = mine_ref[at : at + count] + theirs_ref[at : at + count]
        at += count


def meet_more_kernel(place, mine_ref, theirs_ref, extra_ref, out_ref):
    count = mine_ref.shape[0]
    out_ref[:count] = mine_ref[...] + theirs_ref[...]
    out_ref[count:] = extra_ref[...]


def lead_kernel(place, mine_ref, other_ref, out_ref):
    out_ref[0] = mine_ref[0]
    out_ref[1] = other_ref[0]


def merge_kernel(place, owner_ref, native_ref, received_ref, out_ref):
    own = jnp.logical_or(place[0] == 0, owner_ref[0] == place[0])
    for b in range(out_ref.shape[0]):
        out_ref[b] = jnp.where(own, native_ref[b], received_ref[b])


def merge_or_send_kernel(place, owner_ref, native_ref, received_ref, fresh_ref, out_ref, *, chips):
    own = jnp.logical_or(place[0] == 0, owner_ref[0] == place[0])
    end = jnp.logical_or(place[0] == 0, place[0] == chips - 1)
    for b in range(out_ref.shape[0]):
        merged = jnp.where(own, native_ref[b], received_ref[b])
        out_ref[b] = jnp.where(end, fresh_ref[b], merged)


def finish_kernel(place, owner_ref, me_ref, native_ref, *refs):
    *received, mine_ref, send_ref = refs
    chips = len(received) + 1
    chip = place[0]
    owner = owner_ref[0]
    me = me_ref[0] != 0
    passed = jnp.logical_and(owner == chip, chip != 0)
    passed_mine = jnp.logical_and(passed, me)
    passed_other = jnp.logical_and(passed, jnp.logical_not(me))
    for at in range(chips):

        @pl.when(chip == at)
        def _(at=at):
            for b in range(native_ref.shape[0]):
                native = native_ref[b]
                left = received[at - 1][b] if at > 0 else native
                right = received[chips - 2 - at][b] if at < chips - 1 else native
                new = jnp.where(owner < chip, left, jnp.where(owner > chip, right, native))
                mine_ref[b] = jnp.where(passed_mine, left, new)
                send_ref[b] = jnp.where(passed_other, left, new)


def side_kernel(place, own_ref, down_ref, out_ref):
    out_ref[...] = jnp.where(place[2] < 2, own_ref[...], down_ref[...])


def pair_kernel(place, own_ref, down_ref, side_ref, *out_refs):
    near = jnp.where(place[2] < 2, own_ref[...], down_ref[...])
    even = place[2] % 2 == 0
    first = jnp.where(even, near, side_ref[...])
    second = jnp.where(even, side_ref[...], near)
    for i, out_ref in enumerate(out_refs):
        out_ref[0] = first[i]
        out_ref[1] = second[i]


def placement_kernel(place, lands_ref, put_ref, keep_ref):
    cycles, size, slots = put_ref.shape
    for cycle in range(cycles):
        at = iota((size, size), 0) + cycle * size
        halves = []
        for half in range(2):
            hit = jnp.where(lands_ref[half : half + 1] == at, 1.0, 0.0)
            put_ref[cycle, :, half * size : (half + 1) * size] = hit.astype(BF16)
            halves.append(hit)
        filled = jnp.sum(halves[0] + halves[1], axis=1, keepdims=True)
        keep_ref[cycle] = jnp.broadcast_to(1.0 - filled, (size, size)).astype(BF16)


def placement(chain, place, lands, cycles):
    size = lands.shape[1]
    return chain.whole(
        placement_kernel,
        "placement",
        place,
        (lands,),
        [array(cycles, size, STEPS * size), array(cycles, size, size)],
    )


def three_parts(a):
    high = a.astype(BF16)
    rest = a - high.astype(F32)
    mid = rest.astype(BF16)
    low = (rest - mid.astype(F32)).astype(BF16)
    return jnp.concatenate([low, mid, high], 1)


def sum_parts(a):
    size = a.shape[1] // 3
    return (a[:, :size] + a[:, size : 2 * size]) + a[:, 2 * size :]


def newton_inverse(diag, identity):
    third = 1.0 / 3.0
    approx = (2.0 * identity - diag.astype(F32) * third) * third
    for _ in range(NEWTON - 1):
        product = sum_parts(dot(diag, three_parts(approx)))
        approx = dot_full(approx, 2.0 * identity - product)
    return approx


def whole_rows(place, me_ref, own_mine, own_other, x_mine, x_other):
    mine = jnp.where(me_ref[0] != 0, own_mine, x_mine)
    other = jnp.where(me_ref[1] != 0, own_other, x_other)
    first_core = place[1] == 0
    return jnp.where(first_core, mine, other), jnp.where(first_core, other, mine)


def old_rows(place, x_mine, x_other, top_mine, top_other):
    first_chip = place[0] == 0
    return jnp.concatenate(
        [
            jnp.where(first_chip, top_mine, x_mine),
            jnp.where(first_chip, top_other, x_other),
        ],
        axis=0,
    )


def panel_rows_kernel(place, onehot_ref, *rest):
    *pieces, raw_ref, own_ref, first_ref, sems = rest
    _, cycles, size, _ = raw_ref.shape

    def fetch(first, second):
        copies = [
            pltpu.make_async_copy(source, raw_ref.at[b], sems.at[b])
            for b, source in enumerate((first, second))
        ]
        for copy in copies:
            copy.start()
        for copy in copies:
            copy.wait()

    if len(pieces) == 2:
        fetch(*pieces)
    else:
        own, down, over = pieces
        for col, pair in enumerate(((own, over), (over, own), (down, over), (over, down))):

            @pl.when(place[2] == col)
            def _(pair=pair):
                fetch(*pair)

    flat = [raw_ref[b].reshape(cycles * size, size) for b in range(2)]
    total = dot(onehot_ref[...], jnp.concatenate(flat, 1)).astype(BF16)
    for b in range(2):
        own_ref[b] = total[:, b * size : (b + 1) * size]
        first_ref[b] = raw_ref[b, 0]


def panel_rows(chain, place, onehot, pieces):
    cycles, size, _ = pieces[0].shape
    return chain.run(
        panel_rows_kernel,
        "panel_rows",
        (place, onehot, *pieces),
        [SMEM, VMEM] + [ANY] * len(pieces),
        [
            array(2, cycles, size, size),
            array(2, STEPS * size, size),
            array(2, size, size),
        ],
        [VMEM] * 3,
        scratch_shapes=[pltpu.SemaphoreType.DMA((2,))],
    )


def panel_kernel(
    place, me_ref, xm_ref, xo_ref, top_ref, raw_ref, own_ref, put_ref, keep_ref,
    side_ref, lower1_ref, corner_ref,
):
    _, cycles, size, _ = raw_ref.shape
    row = 2 * place[0] + place[1]
    slots = STEPS * size
    raw0, raw1 = raw_ref.at[0], raw_ref.at[1]
    new0, new1, old = [], [], []
    for b in range(2):
        mine, other = own_ref[b, :size], own_ref[b, size:]
        upper, below = whole_rows(place, me_ref, mine, other, xm_ref[b], xo_ref[b])
        new0.append(upper)
        new1.append(below)
        old.append(old_rows(place, xm_ref[b], xo_ref[b], raw_ref[b, 0], top_ref[b]))
    old = jnp.concatenate(old, 1)
    identity = jnp.where(iota((size, size), 0) == iota((size, size), 1), 1.0, 0.0).astype(F32)
    inverse0 = three_parts(newton_inverse(new0[0], identity))
    corner = sum_parts(dot(new1[0], inverse0)).astype(BF16)
    corner_ref[...] = corner
    inverse1 = three_parts(
        newton_inverse((new1[1].astype(F32) - dot(corner, new0[1])).astype(BF16), identity)
    )
    for cycle in range(cycles):
        put = put_ref[cycle]
        keep = keep_ref[cycle]
        both = dot(put, old)
        left = (both[:, :size] + (keep * raw0[cycle]).astype(F32)).astype(BF16)
        right = both[:, size:] + (keep * raw1[cycle]).astype(F32)
        if cycle == 0:
            left = jnp.where(row == 0, new0[0], jnp.where(row == 1, new1[0], left))
            right = jnp.where(
                row == 0, new0[1].astype(F32), jnp.where(row == 1, new1[1].astype(F32), right)
            )
        lower = sum_parts(dot(left, inverse0))
        if cycle == 0:
            lower = jnp.where(row == 0, 0.0, lower)
        lower = lower.astype(BF16)
        side_ref[cycle, :, :slots] = put
        side_ref[cycle, :, slots:] = -lower
        right = (right - dot(lower, new0[1])).astype(BF16)
        lower = sum_parts(dot(right, inverse1))
        if cycle == 0:
            lower = jnp.where(row <= 1, 0.0, lower)
        lower1_ref[cycle] = lower.astype(BF16)


def factor_panels(chain, place, me, rows, tops, raw, own, put, keep):
    cycles, size, _ = keep.shape
    return chain.run(
        panel_kernel,
        "factor_panels",
        (place, me, *rows, tops, raw, own, put, keep),
        [SMEM] + [VMEM] * 8,
        [
            array(cycles, size, (STEPS + 1) * size),
            array(cycles, size, size),
            array(size, size),
        ],
        [VMEM] * 3,
    )


def update_kernel(first, counts, place, me_ref, block_ref, top_ref, *rest):
    sets = [rest[4 * i : 4 * i + 4] for i in range(len(counts))]
    side_ref, keep_ref, lower1_ref, corner_ref = rest[4 * len(counts) : 4 * len(counts) + 4]
    out_ref, both_ref, below_ref = rest[-3:]
    cycles, width, size, _ = block_ref.shape
    at = pl.program_id(0) * width
    row = 2 * place[0] + place[1]
    slots = STEPS * size
    start = 0
    for (native_ref, own_ref, xm_ref, xo_ref), count in zip(sets, counts):

        def prepare(start=start, native_ref=native_ref, own_ref=own_ref, xm_ref=xm_ref, xo_ref=xo_ref):
            for b in range(width):
                i = at + (b - start)
                xm, xo = xm_ref[i], xo_ref[i]
                upper, below = whole_rows(place, me_ref, native_ref[i], own_ref[i], xm, xo)
                old = old_rows(place, xm, xo, block_ref[0, b], top_ref[b])
                part = slice(b * size, (b + 1) * size)
                both_ref[:slots, part] = old
                both_ref[slots:, part] = upper
                below_ref[:, part] = below

        if len(counts) == 1:
            prepare()
        else:
            pl.when(jnp.logical_and(at >= start, at < start + count))(prepare)
        start += count
    join = lambda parts: parts[0] if width == 1 else jnp.concatenate(parts, 1)
    both = both_ref[...]
    upper = both[slots:]
    upper1 = (below_ref[...].astype(F32) - dot(corner_ref[...], upper)).astype(BF16)
    for cycle in range(cycles):
        keep = keep_ref[cycle]
        kept = join([block_ref[cycle, b] * keep for b in range(width)])
        block = (dot(side_ref[cycle], both) + kept.astype(F32)).astype(BF16)
        if cycle == 0:
            block = jnp.where(row == 0, upper, jnp.where(row == 1, upper1, block))
        block = (block.astype(F32) - dot(lower1_ref[cycle], upper1)).astype(BF16)
        for b in range(width):
            out_ref[cycle, b] = block[:, b * size : (b + 1) * size]
    if first == 0:

        @pl.when(jnp.logical_and(pl.program_id(0) == 0, place[2] == 0))
        def _():
            for cycle in range(cycles):
                block = -side_ref[cycle, :, slots:]
                if cycle == 0:
                    block = jnp.where(row == 0, upper[:, :size], block)
                out_ref[cycle, 0] = block

        @pl.when(jnp.logical_and(pl.program_id(0) == 0, place[2] == 1))
        def _():
            for cycle in range(cycles):
                block = lower1_ref[cycle]
                if cycle == 0:
                    block = jnp.where(
                        row == 0, upper[:, :size], jnp.where(row == 1, upper1[:, :size], block)
                    )
                out_ref[cycle, 0] = block


def update_columns(chain, place, me, matrix, sets, top, factors, first, width, result):
    cycles, blocks, size, _ = matrix.shape
    counts = [s[0].shape[0] for s in sets]
    rows = [r for s in sets for r in s]
    at = lambda j: j + first // width
    blocks_spec = pl.BlockSpec((cycles, width, size, size), lambda j: (0, at(j), 0, 0))
    top_spec = pl.BlockSpec((width, size, size), lambda j: (at(j), 0, 0))
    operands = [place, me, matrix, top, *rows, *factors]
    in_specs = [SMEM, VMEM, blocks_spec, top_spec]
    in_specs += [VMEM] * (len(rows) + len(factors))
    aliases = {}
    if result is not None:
        aliases = {len(operands): 0}
        operands.append(result)
        in_specs.append(ANY)
    return chain.run(
        functools.partial(update_kernel, first, counts),
        "update_columns",
        operands,
        in_specs,
        [array(*matrix.shape)],
        [blocks_spec],
        grid=(sum(counts) // width,),
        scratch_shapes=[
            pltpu.VMEM(((STEPS + 1) * size, width * size), BF16),
            pltpu.VMEM((size, width * size), BF16),
        ],
        input_output_aliases=aliases,
    )[0]


def split_blocks(blocks):
    width = 2 if blocks % 2 == 0 else 1
    base, extra = divmod(blocks // width - 1, 3)
    counts = [width] + [width * (base + (1 if i < extra else 0)) for i in range(3)]
    return width, [(sum(counts[:i]), c) for i, c in enumerate(counts)]


def body(matrix, pivots):
    rows = lax.axis_size("row")
    cols = lax.axis_size("col")
    chips = rows // 2
    row = lax.axis_index("row")
    col = lax.axis_index("col")
    cycles, size, blocks, _ = matrix.shape
    plain = matrix.transpose(0, 2, 1, 3)
    matrix = pltpu.with_memory_space_constraint(plain, pltpu.HBM)
    place = jnp.stack([row // 2, row % 2, col]).astype(I32)
    width, chunks = split_blocks(blocks)
    count = len(chunks)
    few_cols = cols == 4

    swap = [(r, r ^ 1) for r in range(rows)]
    first_swap = [(0, 1), (1, 0)]
    down_pairs = [(0, 2), (1, 3)]
    side_pairs = [(0, 1), (1, 0), (2, 3), (3, 2)]

    def hop_pairs(h):
        pairs = []
        for a, b in ((h, h + 1), (chips - 1 - h, chips - 2 - h)):
            pairs += [(2 * a, 2 * b), (2 * a + 1, 2 * b + 1)]
        return pairs

    onehot, owner, me, lands, raw, mine, other, top, token = start(
        place, pivots, matrix, width, rows
    )
    chain = Chain(token)
    native, others, x_mine, x_send, x_other = {}, {}, {}, {}, {}
    hops = {i: [] for i in range(count)}

    def exchange(own):
        return lax.ppermute(own, "row", swap)

    def gather(i, blocks):
        return gather_rows(chain, matrix, onehot, chunks[i][0], blocks, width)

    def meet(mine, theirs, *counts):
        return chain.whole(
            meet_kernel, "meet", place, (mine, theirs), [array(c, size, size) for c in counts]
        )

    def hop_part(i):
        h = len(hops[i])
        shape = array(*native[i].shape)

        def go(out):
            hops[i].append(lax.ppermute(out[0], "row", hop_pairs(h)))

        return merge_kernel, (owner, native[i], hops[i][-1]), [shape], go

    def both_part(i, j):
        if chips != 4 or native[i].shape != native[j].shape:
            hop(j)
            return hop_part(i)

        def go(out):
            arrived = lax.ppermute(out[0], "row", hop_pairs(0) + hop_pairs(2))
            hops[i].append(arrived)
            hops[j].append(arrived)

        kernel = functools.partial(merge_or_send_kernel, chips=chips)
        operands = (owner, native[i], hops[i][-1], native[j])
        return kernel, operands, [array(*native[i].shape)], go

    def finish_part(i):
        while len(hops[i]) < chips - 1:
            hop(i)

        def go(out):
            x_mine[i], x_send[i] = out
            x_other[i] = exchange(x_send[i])

        operands = (owner, me, native[i], *hops[i])
        return finish_kernel, operands, [array(*native[i].shape)] * 2, go

    def meet_part(i, mine, theirs):
        def go(out):
            (native[i],) = out

        return meet_kernel, (mine, theirs), [array(*mine.shape)], go

    def group(*parts):
        outs = chain.together(place, [part[:3] for part in parts])
        for part, out in zip(parts, outs):
            part[3](out)

    def hop(i):
        if hops[i]:
            group(hop_part(i))
        else:
            hops[i].append(lax.ppermute(native[i], "row", hop_pairs(0)))

    def finish(i):
        group(finish_part(i))

    def side(own, down):
        (out,) = chain.whole(side_kernel, "side", place, (own, down), [array(*own.shape)])
        return lax.ppermute(out, "col", side_pairs)

    def down(own):
        return lax.ppermute(own, "col", down_pairs)

    def pair(own, down, side, made):
        return chain.whole(
            pair_kernel, "pair", place, (own, down, side), [array(2, size, size)] * made
        )

    def from_two(own):
        zero = jnp.zeros_like(own)
        return lax.psum(jnp.stack([jnp.where(col == b, own, zero) for b in range(2)]), "col")

    native[0], others[0] = mine, other
    theirs0 = exchange(other)
    if few_cols:
        down_raw = down(raw)
    sizes = [c for _, c in chunks]
    cut = sizes[1]
    some_mine, some_other = gather(1, sizes[1] + sizes[2])
    chain.hold(some_other)
    (native[0],) = meet(mine, theirs0, width)
    (some_other,) = chain.passed
    hop(0)
    some_theirs = exchange(some_other)
    others[1], others[2] = some_other[:cut], some_other[cut:]
    mine3, others[3] = gather(3, sizes[3])
    chain.hold(others[3])
    native[1], native[2] = meet(some_mine, some_theirs, sizes[1], sizes[2])
    (others[3],) = chain.passed
    hop(1)
    theirs3 = exchange(others[3])
    chain.hold(native[2])
    hop(0)
    (native[2],) = chain.passed
    hop(2)
    put, keep = placement(chain, place, lands, cycles)
    if few_cols:
        side_raw = side(raw, down_raw)
    chain.hold(top)
    group(hop_part(0), hop_part(1), meet_part(3, mine3, theirs3))
    (top,) = chain.passed
    top = lax.ppermute(top, "row", first_swap)
    finish(0)
    (lead,) = chain.whole(
        lead_kernel, "lead", place, (x_mine[0], x_other[0]), [array(2, size, size)]
    )
    if few_cols:
        down_lead = down(lead)
    else:
        leads = from_two(lead)
    group(hop_part(2), both_part(1, 3))
    if few_cols:
        pieces = [raw, down_raw, side_raw]
    else:
        raws = from_two(raw)
        pieces = [raws[0], raws[1]]
    panels, panel_own, firsts = panel_rows(chain, place, onehot, pieces)
    tops = lax.ppermute(firsts, "row", first_swap)
    if few_cols:
        side_lead = side(lead, down_lead)
    if few_cols:
        panel_mine, panel_other = pair(lead, down_lead, side_lead, 2)
    else:
        panel_mine, panel_other = leads[:, 0], leads[:, 1]
    group(hop_part(2), hop_part(3), finish_part(1))
    side_rows, lower1, corner = factor_panels(
        chain, place, me, (panel_mine, panel_other), tops, panels, panel_own, put, keep
    )
    factors = (side_rows, keep, lower1, corner)

    def update(which, result):
        sets = [(native[i], others[i], x_mine[i], x_other[i]) for i in which]
        return update_columns(
            chain, place, me, matrix, sets, top, factors, chunks[which[0]][0], width, result
        )

    group(hop_part(3), finish_part(2))
    result = update((0, 1, 2), None)
    finish(3)
    result = update((3,), result)
    return result.transpose(0, 2, 1, 3)


def solution(mesh):
    return jax.shard_map(
        body,
        mesh=mesh,
        in_specs=(P(None, "row", None, "col"), P()),
        out_specs=P(None, "row", None, "col"),
        check_vma=False,
    )
```

```python
import functools

import jax
import jax.numpy as jnp
from jax import lax
from jax.experimental import pallas as pl
from jax.experimental.pallas import tpu as pltpu
from jax.sharding import PartitionSpec as P

STEPS = 2
NEWTON = 3
F32 = jnp.float32
BF16 = jnp.bfloat16
I32 = jnp.int32
VMEM_LIMIT = 24 * 1024 * 1024
CHEAP = pl.CostEstimate(flops=1024, bytes_accessed=1024, transcendentals=0)
ANY = pl.BlockSpec(memory_space=pl.ANY)
SMEM = pl.BlockSpec(memory_space=pltpu.SMEM)
VMEM = pl.BlockSpec(memory_space=pltpu.VMEM)


def dot(a, b):
    return jnp.dot(a, b, preferred_element_type=F32)


def dot_full(a, b):
    return jnp.dot(a, b, precision=lax.Precision.HIGHEST, preferred_element_type=F32)


def params():
    return pltpu.CompilerParams(vmem_limit_bytes=VMEM_LIMIT)


def iota(shape, dim):
    return lax.broadcasted_iota(I32, shape, dim)


def to_column(row):
    size = row.shape[1]
    diagonal = iota((size, size), 0) == iota((size, size), 1)
    return jnp.sum(jnp.where(diagonal, row.astype(F32), 0.0), axis=1, keepdims=True).astype(I32)


def to_row(column):
    size = column.shape[0]
    diagonal = iota((size, size), 0) == iota((size, size), 1)
    return jnp.sum(jnp.where(diagonal, column.astype(F32), 0.0), axis=0, keepdims=True).astype(I32)


def pick_sum(mask, value, axis):
    return jnp.sum(jnp.where(mask, value.astype(F32), 0.0), axis=axis, keepdims=True).astype(I32)


def start_kernel(
    rows, place, pivot_ref, matrix_ref, block_ref,
    onehot_ref, owner_ref, me_ref, lands_ref, raw_ref, mine_ref, other_ref, top_ref, token_ref, sem,
):
    copy = pltpu.make_async_copy(matrix_ref.at[0], top_ref, sem)
    copy.start()
    cycles, width, size, _ = block_ref.shape
    chip, core = place[0], place[1]
    row = 2 * chip + core

    @pl.when(pl.program_id(0) == 0)
    def _():
        square = (size, size)
        pivot0, pivot1 = pivot_ref[0:1], pivot_ref[1:2]
        column0 = to_column(pivot0)
        down, across = iota(square, 0), iota(square, 1)
        again = column0 == pivot1
        inner = column0 == across + size
        at = iota((1, size), 1)
        second = size + at + pick_sum(inner, down - across - size, 0)
        source1 = pivot1 + pick_sum(again, down - pivot1, 0)
        leaves0 = iota((size, 1), 0) + pick_sum(again, second - down, 1)
        device_of = lambda r: r // size % rows
        local_of = lambda r: r // (size * rows) * size + r % size

        def of_slots(source, leaves):
            device = device_of(source)
            owner = device // 2
            me = device == row
            come = jnp.where(jnp.logical_and(chip == 0, owner != 0), leaves, source)
            taken = jnp.where(device_of(come) == row, local_of(come), -1)
            return owner, me.astype(I32), taken

        first = of_slots(column0, leaves0)
        last = of_slots(to_column(source1), to_column(second))
        swapped = core == 1
        mine = [jnp.where(swapped, b, a) for a, b in zip(first, last)]
        other = [jnp.where(swapped, a, b) for a, b in zip(first, last)]
        for half, values in enumerate((mine, other)):
            owner_ref[half] = values[0]
            me_ref[half] = values[1]
            for cycle in range(cycles):
                hit = values[2] == across + cycle * size
                onehot_ref[half * size : (half + 1) * size, cycle * size : (cycle + 1) * size] = (
                    jnp.where(hit, 1.0, 0.0).astype(BF16)
                )

        slots = STEPS * size
        lands = []
        for source in (pivot0, source1):
            outside = jnp.logical_and(device_of(source) == row, source >= slots)
            lands.append(jnp.where(outside, local_of(source), -1))
        by_top = []
        leaving = (leaves0, to_column(second))
        landing = [to_column(v) for v in lands]
        for half in range(2):
            total = jnp.full((1, size), -1, I32)
            for leave, land in zip(leaving, landing):
                total += pick_sum(leave == across + half * size, land + 1, 0)
            by_top.append(total)
        lands = [jnp.where(chip == 0, a, b) for a, b in zip(by_top, lands)]
        lands_ref[0:1] = jnp.where(swapped, lands[1], lands[0])
        lands_ref[1:2] = jnp.where(swapped, lands[0], lands[1])
        raw_ref[...] = block_ref[:, 0]

    gather_step(onehot_ref, block_ref, mine_ref, other_ref)
    copy.wait()


def gather_step(onehot_ref, block_ref, mine_ref, other_ref):
    cycles, width, size, _ = block_ref.shape
    columns = [
        jnp.concatenate([block_ref[cycle, b] for cycle in range(cycles)], 0) for b in range(width)
    ]
    columns = columns[0] if width == 1 else jnp.concatenate(columns, 1)
    total = dot(onehot_ref[...], columns).astype(BF16)
    for b in range(width):
        mine_ref[b] = total[:size, b * size : (b + 1) * size]
        other_ref[b] = total[size:, b * size : (b + 1) * size]


def constant(shape):
    return pl.BlockSpec(
        shape, lambda *j, n=len(shape): (0,) * n, pipeline_mode=pl.Buffered(1)
    )


def array(*shape, dtype=BF16):
    return jax.ShapeDtypeStruct(shape, dtype)


TOKEN = array(8, 128, dtype=F32)


def start(place, pivots, matrix, width, rows):
    cycles, blocks, size, _ = matrix.shape
    slots = STEPS * size
    part = array(width, size, size)
    outs = [
        array(slots, cycles * size),
        array(2, size, 1, dtype=I32),
        array(2, size, 1, dtype=I32),
        array(2, size, dtype=I32),
        array(cycles, size, size),
        part,
        part,
    ]
    return pl.pallas_call(
        functools.partial(start_kernel, rows),
        grid=(1,),
        in_specs=[
            SMEM,
            constant(pivots.shape),
            ANY,
            pl.BlockSpec((cycles, width, size, size), lambda j: (0, 0, 0, 0)),
        ],
        out_specs=[constant(o.shape) for o in outs] + [ANY, ANY],
        out_shape=outs + [array(blocks, size, size), TOKEN],
        scratch_shapes=[pltpu.SemaphoreType.DMA],
        compiler_params=params(),
        cost_estimate=CHEAP,
        name="start",
    )(place, pivots, matrix, matrix)


class Chain:
    def __init__(self, token):
        self.token = token
        self.due = []
        self.held = []

    def hold(self, *arrays):
        self.held = list(arrays)

    def need(self, *arrays):
        self.due += arrays

    def run(self, kernel, name, operands, in_specs, out_shape, out_specs, **options):
        operands, in_specs = list(operands), list(in_specs)
        given, made = len(operands), len(out_shape)
        held, waits = self.held, [self.token, *self.due]
        self.due, self.held = [], []
        aliases = dict(options.pop("input_output_aliases", {}))
        for i in range(len(held)):
            aliases[given + len(waits) + i] = made + 1 + i
        passed = len(held)

        def inner(*refs):
            outs = given + len(waits) + passed
            kernel(*refs[:given], *refs[outs : outs + made], *refs[outs + made + 1 + passed :])

        outs = pl.pallas_call(
            inner,
            in_specs=in_specs + [ANY] * (len(waits) + passed),
            out_specs=list(out_specs) + [ANY] * (1 + passed),
            out_shape=list(out_shape) + [TOKEN] + [array(*a.shape) for a in held],
            input_output_aliases=aliases,
            compiler_params=params(),
            cost_estimate=CHEAP,
            name=name,
            **options,
        )(*operands, *waits, *held)
        self.token, self.passed = outs[made], outs[made + 1 :]
        return outs[:made]

    def whole(self, kernel, name, place, operands, out_shape, **options):
        return self.run(
            kernel,
            name,
            (place, *operands),
            [SMEM] + [VMEM] * len(operands),
            out_shape,
            [VMEM] * len(out_shape),
            **options,
        )


    def together(self, place, parts):
        def kernel(place_ref, *refs):
            at, made = 0, sum(len(part[1]) for part in parts)
            for part, operands, shapes in parts:
                part(place_ref, *refs[at : at + len(operands)], *refs[made : made + len(shapes)])
                at += len(operands)
                made += len(shapes)

        name = "_".join(getattr(part[0], "func", part[0]).__name__[:-7] for part in parts)
        outs = self.whole(
            kernel,
            name,
            place,
            [operand for part in parts for operand in part[1]],
            [shape for part in parts for shape in part[2]],
        )
        split, at = [], 0
        for part in parts:
            split.append(outs[at : at + len(part[2])])
            at += len(part[2])
        return split


def gather_rows(chain, matrix, onehot, first, count, width):
    cycles, _, size, _ = matrix.shape
    part = array(count, size, size)
    part_spec = pl.BlockSpec((width, size, size), lambda j: (j, 0, 0))
    return chain.run(
        gather_step,
        "gather_rows",
        (onehot, matrix),
        [
            VMEM,
            pl.BlockSpec((cycles, width, size, size), lambda j: (0, j + first // width, 0, 0)),
        ],
        [part, part],
        [part_spec, part_spec],
        grid=(count // width,),
    )


def meet_kernel(place, mine_ref, theirs_ref, *out_refs):
    at = 0
    for out_ref in out_refs:
        count = out_ref.shape[0]
        out_ref[...] = mine_ref[at : at + count] + theirs_ref[at : at + count]
        at += count


def meet_more_kernel(place, mine_ref, theirs_ref, extra_ref, out_ref):
    count = mine_ref.shape[0]
    out_ref[:count] = mine_ref[...] + theirs_ref[...]
    out_ref[count:] = extra_ref[...]


def lead_kernel(place, mine_ref, other_ref, out_ref):
    out_ref[0] = mine_ref[0]
    out_ref[1] = other_ref[0]


def merge_kernel(place, owner_ref, native_ref, received_ref, out_ref):
    own = jnp.logical_or(place[0] == 0, owner_ref[0] == place[0])
    for b in range(out_ref.shape[0]):
        out_ref[b] = jnp.where(own, native_ref[b], received_ref[b])


def merge_or_send_kernel(place, owner_ref, native_ref, received_ref, fresh_ref, out_ref, *, chips):
    own = jnp.logical_or(place[0] == 0, owner_ref[0] == place[0])
    end = jnp.logical_or(place[0] == 0, place[0] == chips - 1)
    for b in range(out_ref.shape[0]):
        merged = jnp.where(own, native_ref[b], received_ref[b])
        out_ref[b] = jnp.where(end, fresh_ref[b], merged)


def finish_kernel(place, owner_ref, me_ref, native_ref, *refs):
    *received, mine_ref, send_ref = refs
    chips = len(received) + 1
    chip = place[0]
    owner = owner_ref[0]
    me = me_ref[0] != 0
    passed = jnp.logical_and(owner == chip, chip != 0)
    passed_mine = jnp.logical_and(passed, me)
    passed_other = jnp.logical_and(passed, jnp.logical_not(me))
    for at in range(chips):

        @pl.when(chip == at)
        def _(at=at):
            for b in range(native_ref.shape[0]):
                native = native_ref[b]
                left = received[at - 1][b] if at > 0 else native
                right = received[chips - 2 - at][b] if at < chips - 1 else native
                new = jnp.where(owner < chip, left, jnp.where(owner > chip, right, native))
                mine_ref[b] = jnp.where(passed_mine, left, new)
                send_ref[b] = jnp.where(passed_other, left, new)


def side_kernel(place, own_ref, down_ref, out_ref):
    out_ref[...] = jnp.where(place[2] < 2, own_ref[...], down_ref[...])


def pair_kernel(place, own_ref, down_ref, side_ref, *out_refs):
    near = jnp.where(place[2] < 2, own_ref[...], down_ref[...])
    even = place[2] % 2 == 0
    first = jnp.where(even, near, side_ref[...])
    second = jnp.where(even, side_ref[...], near)
    for i, out_ref in enumerate(out_refs):
        out_ref[0] = first[i]
        out_ref[1] = second[i]


def placement_kernel(place, lands_ref, put_ref, keep_ref):
    cycles, size, slots = put_ref.shape
    for cycle in range(cycles):
        at = iota((size, size), 0) + cycle * size
        halves = []
        for half in range(2):
            hit = jnp.where(lands_ref[half : half + 1] == at, 1.0, 0.0)
            put_ref[cycle, :, half * size : (half + 1) * size] = hit.astype(BF16)
            halves.append(hit)
        filled = jnp.sum(halves[0] + halves[1], axis=1, keepdims=True)
        keep_ref[cycle] = jnp.broadcast_to(1.0 - filled, (size, size)).astype(BF16)


def placement(chain, place, lands, cycles):
    size = lands.shape[1]
    return chain.whole(
        placement_kernel,
        "placement",
        place,
        (lands,),
        [array(cycles, size, STEPS * size), array(cycles, size, size)],
    )


def three_parts(a):
    high = a.astype(BF16)
    rest = a - high.astype(F32)
    mid = rest.astype(BF16)
    low = (rest - mid.astype(F32)).astype(BF16)
    return jnp.concatenate([low, mid, high], 1)


def sum_parts(a):
    size = a.shape[1] // 3
    return (a[:, :size] + a[:, size : 2 * size]) + a[:, 2 * size :]


def newton_inverse(diag, identity):
    third = 1.0 / 3.0
    approx = (2.0 * identity - diag.astype(F32) * third) * third
    for _ in range(NEWTON - 1):
        product = sum_parts(dot(diag, three_parts(approx)))
        approx = dot_full(approx, 2.0 * identity - product)
    return approx


def whole_rows(place, me_ref, own_mine, own_other, x_mine, x_other):
    mine = jnp.where(me_ref[0] != 0, own_mine, x_mine)
    other = jnp.where(me_ref[1] != 0, own_other, x_other)
    first_core = place[1] == 0
    return jnp.where(first_core, mine, other), jnp.where(first_core, other, mine)


def old_rows(place, x_mine, x_other, top_mine, top_other):
    first_chip = place[0] == 0
    return jnp.concatenate(
        [
            jnp.where(first_chip, top_mine, x_mine),
            jnp.where(first_chip, top_other, x_other),
        ],
        axis=0,
    )


def panel_rows_kernel(place, onehot_ref, *rest):
    *pieces, raw_ref, own_ref, first_ref, sems = rest
    _, cycles, size, _ = raw_ref.shape

    def fetch(first, second):
        copies = [
            pltpu.make_async_copy(source, raw_ref.at[b], sems.at[b])
            for b, source in enumerate((first, second))
        ]
        for copy in copies:
            copy.start()
        for copy in copies:
            copy.wait()

    if len(pieces) == 2:
        fetch(*pieces)
    else:
        own, down, over = pieces
        for col, pair in enumerate(((own, over), (over, own), (down, over), (over, down))):

            @pl.when(place[2] == col)
            def _(pair=pair):
                fetch(*pair)

    flat = [raw_ref[b].reshape(cycles * size, size) for b in range(2)]
    total = dot(onehot_ref[...], jnp.concatenate(flat, 1)).astype(BF16)
    for b in range(2):
        own_ref[b] = total[:, b * size : (b + 1) * size]
        first_ref[b] = raw_ref[b, 0]


def panel_rows(chain, place, onehot, pieces):
    cycles, size, _ = pieces[0].shape
    return chain.run(
        panel_rows_kernel,
        "panel_rows",
        (place, onehot, *pieces),
        [SMEM, VMEM] + [ANY] * len(pieces),
        [
            array(2, cycles, size, size),
            array(2, STEPS * size, size),
            array(2, size, size),
        ],
        [VMEM] * 3,
        scratch_shapes=[pltpu.SemaphoreType.DMA((2,))],
    )


def panel_kernel(
    place, me_ref, xm_ref, xo_ref, top_ref, raw_ref, own_ref, put_ref, keep_ref,
    side_ref, lower1_ref, corner_ref,
):
    _, cycles, size, _ = raw_ref.shape
    row = 2 * place[0] + place[1]
    slots = STEPS * size
    raw0, raw1 = raw_ref.at[0], raw_ref.at[1]
    new0, new1, old = [], [], []
    for b in range(2):
        mine, other = own_ref[b, :size], own_ref[b, size:]
        upper, below = whole_rows(place, me_ref, mine, other, xm_ref[b], xo_ref[b])
        new0.append(upper)
        new1.append(below)
        old.append(old_rows(place, xm_ref[b], xo_ref[b], raw_ref[b, 0], top_ref[b]))
    old = jnp.concatenate(old, 1)
    identity = jnp.where(iota((size, size), 0) == iota((size, size), 1), 1.0, 0.0).astype(F32)
    inverse0 = three_parts(newton_inverse(new0[0], identity))
    corner = sum_parts(dot(new1[0], inverse0)).astype(BF16)
    corner_ref[...] = corner
    inverse1 = three_parts(
        newton_inverse((new1[1].astype(F32) - dot(corner, new0[1])).astype(BF16), identity)
    )
    for cycle in range(cycles):
        put = put_ref[cycle]
        keep = keep_ref[cycle]
        both = dot(put, old)
        left = (both[:, :size] + (keep * raw0[cycle]).astype(F32)).astype(BF16)
        right = both[:, size:] + (keep * raw1[cycle]).astype(F32)
        if cycle == 0:
            left = jnp.where(row == 0, new0[0], jnp.where(row == 1, new1[0], left))
            right = jnp.where(
                row == 0, new0[1].astype(F32), jnp.where(row == 1, new1[1].astype(F32), right)
            )
        lower = sum_parts(dot(left, inverse0))
        if cycle == 0:
            lower = jnp.where(row == 0, 0.0, lower)
        lower = lower.astype(BF16)
        side_ref[cycle, :, :slots] = put
        side_ref[cycle, :, slots:] = -lower
        right = (right - dot(lower, new0[1])).astype(BF16)
        lower = sum_parts(dot(right, inverse1))
        if cycle == 0:
            lower = jnp.where(row <= 1, 0.0, lower)
        lower1_ref[cycle] = lower.astype(BF16)


def factor_panels(chain, place, me, rows, tops, raw, own, put, keep):
    cycles, size, _ = keep.shape
    return chain.run(
        panel_kernel,
        "factor_panels",
        (place, me, *rows, tops, raw, own, put, keep),
        [SMEM] + [VMEM] * 8,
        [
            array(cycles, size, (STEPS + 1) * size),
            array(cycles, size, size),
            array(size, size),
        ],
        [VMEM] * 3,
    )


def update_kernel(first, counts, place, me_ref, block_ref, top_ref, *rest):
    sets = [rest[4 * i : 4 * i + 4] for i in range(len(counts))]
    side_ref, keep_ref, lower1_ref, corner_ref = rest[4 * len(counts) : 4 * len(counts) + 4]
    out_ref, both_ref, below_ref = rest[-3:]
    cycles, width, size, _ = block_ref.shape
    at = pl.program_id(0) * width
    row = 2 * place[0] + place[1]
    slots = STEPS * size
    start = 0
    for (native_ref, own_ref, xm_ref, xo_ref), count in zip(sets, counts):

        def prepare(start=start, native_ref=native_ref, own_ref=own_ref, xm_ref=xm_ref, xo_ref=xo_ref):
            for b in range(width):
                i = at + (b - start)
                xm, xo = xm_ref[i], xo_ref[i]
                upper, below = whole_rows(place, me_ref, native_ref[i], own_ref[i], xm, xo)
                old = old_rows(place, xm, xo, block_ref[0, b], top_ref[b])
                part = slice(b * size, (b + 1) * size)
                both_ref[:slots, part] = old
                both_ref[slots:, part] = upper
                below_ref[:, part] = below

        if len(counts) == 1:
            prepare()
        else:
            pl.when(jnp.logical_and(at >= start, at < start + count))(prepare)
        start += count
    join = lambda parts: parts[0] if width == 1 else jnp.concatenate(parts, 1)
    both = both_ref[...]
    upper = both[slots:]
    upper1 = (below_ref[...].astype(F32) - dot(corner_ref[...], upper)).astype(BF16)
    for cycle in range(cycles):
        keep = keep_ref[cycle]
        kept = join([block_ref[cycle, b] * keep for b in range(width)])
        block = (dot(side_ref[cycle], both) + kept.astype(F32)).astype(BF16)
        if cycle == 0:
            block = jnp.where(row == 0, upper, jnp.where(row == 1, upper1, block))
        block = (block.astype(F32) - dot(lower1_ref[cycle], upper1)).astype(BF16)
        for b in range(width):
            out_ref[cycle, b] = block[:, b * size : (b + 1) * size]
    if first == 0:

        @pl.when(jnp.logical_and(pl.program_id(0) == 0, place[2] == 0))
        def _():
            for cycle in range(cycles):
                block = -side_ref[cycle, :, slots:]
                if cycle == 0:
                    block = jnp.where(row == 0, upper[:, :size], block)
                out_ref[cycle, 0] = block

        @pl.when(jnp.logical_and(pl.program_id(0) == 0, place[2] == 1))
        def _():
            for cycle in range(cycles):
                block = lower1_ref[cycle]
                if cycle == 0:
                    block = jnp.where(
                        row == 0, upper[:, :size], jnp.where(row == 1, upper1[:, :size], block)
                    )
                out_ref[cycle, 0] = block


def update_columns(chain, place, me, matrix, sets, top, factors, first, width, result):
    cycles, blocks, size, _ = matrix.shape
    counts = [s[0].shape[0] for s in sets]
    rows = [r for s in sets for r in s]
    at = lambda j: j + first // width
    blocks_spec = pl.BlockSpec((cycles, width, size, size), lambda j: (0, at(j), 0, 0))
    top_spec = pl.BlockSpec((width, size, size), lambda j: (at(j), 0, 0))
    operands = [place, me, matrix, top, *rows, *factors]
    in_specs = [SMEM, VMEM, blocks_spec, top_spec]
    in_specs += [VMEM] * (len(rows) + len(factors))
    aliases = {}
    if result is not None:
        aliases = {len(operands): 0}
        operands.append(result)
        in_specs.append(ANY)
    return chain.run(
        functools.partial(update_kernel, first, counts),
        "update_columns",
        operands,
        in_specs,
        [array(*matrix.shape)],
        [blocks_spec],
        grid=(sum(counts) // width,),
        scratch_shapes=[
            pltpu.VMEM(((STEPS + 1) * size, width * size), BF16),
            pltpu.VMEM((size, width * size), BF16),
        ],
        input_output_aliases=aliases,
    )[0]


def split_blocks(blocks):
    width = 2 if blocks % 2 == 0 else 1
    base, extra = divmod(blocks // width - 1, 3)
    counts = [width] + [width * (base + (1 if i < extra else 0)) for i in range(3)]
    return width, [(sum(counts[:i]), c) for i, c in enumerate(counts)]


def body(matrix, pivots):
    rows = lax.axis_size("row")
    cols = lax.axis_size("col")
    chips = rows // 2
    row = lax.axis_index("row")
    col = lax.axis_index("col")
    cycles, size, blocks, _ = matrix.shape
    plain = matrix.transpose(0, 2, 1, 3)
    matrix = pltpu.with_memory_space_constraint(plain, pltpu.HBM)
    place = jnp.stack([row // 2, row % 2, col]).astype(I32)
    width, chunks = split_blocks(blocks)
    count = len(chunks)
    few_cols = cols == 4

    swap = [(r, r ^ 1) for r in range(rows)]
    first_swap = [(0, 1), (1, 0)]
    down_pairs = [(0, 2), (1, 3)]
    side_pairs = [(0, 1), (1, 0), (2, 3), (3, 2)]

    def hop_pairs(h):
        pairs = []
        for a, b in ((h, h + 1), (chips - 1 - h, chips - 2 - h)):
            pairs += [(2 * a, 2 * b), (2 * a + 1, 2 * b + 1)]
        return pairs

    onehot, owner, me, lands, raw, mine, other, top, token = start(
        place, pivots, matrix, width, rows
    )
    chain = Chain(token)
    native, others, x_mine, x_send, x_other = {}, {}, {}, {}, {}
    hops = {i: [] for i in range(count)}

    def exchange(own):
        return lax.ppermute(own, "row", swap)

    def gather(i, blocks):
        return gather_rows(chain, matrix, onehot, chunks[i][0], blocks, width)

    def meet(mine, theirs, *counts):
        return chain.whole(
            meet_kernel, "meet", place, (mine, theirs), [array(c, size, size) for c in counts]
        )

    def hop_part(i):
        h = len(hops[i])
        shape = array(*native[i].shape)

        def go(out):
            hops[i].append(lax.ppermute(out[0], "row", hop_pairs(h)))

        return merge_kernel, (owner, native[i], hops[i][-1]), [shape], go

    def both_part(i, j):
        if chips != 4 or native[i].shape != native[j].shape:
            hop(j)
            return hop_part(i)

        def go(out):
            arrived = lax.ppermute(out[0], "row", hop_pairs(0) + hop_pairs(2))
            hops[i].append(arrived)
            hops[j].append(arrived)

        kernel = functools.partial(merge_or_send_kernel, chips=chips)
        operands = (owner, native[i], hops[i][-1], native[j])
        return kernel, operands, [array(*native[i].shape)], go

    def finish_part(i):
        while len(hops[i]) < chips - 1:
            hop(i)

        def go(out):
            x_mine[i], x_send[i] = out
            x_other[i] = exchange(x_send[i])

        operands = (owner, me, native[i], *hops[i])
        return finish_kernel, operands, [array(*native[i].shape)] * 2, go

    def meet_part(i, mine, theirs):
        def go(out):
            (native[i],) = out

        return meet_kernel, (mine, theirs), [array(*mine.shape)], go

    def group(*parts):
        outs = chain.together(place, [part[:3] for part in parts])
        for part, out in zip(parts, outs):
            part[3](out)

    def hop(i):
        if hops[i]:
            group(hop_part(i))
        else:
            hops[i].append(lax.ppermute(native[i], "row", hop_pairs(0)))

    def finish(i):
        group(finish_part(i))

    def side(own, down):
        (out,) = chain.whole(side_kernel, "side", place, (own, down), [array(*own.shape)])
        return lax.ppermute(out, "col", side_pairs)

    def down(own):
        return lax.ppermute(own, "col", down_pairs)

    def pair(own, down, side, made):
        return chain.whole(
            pair_kernel, "pair", place, (own, down, side), [array(2, size, size)] * made
        )

    def from_two(own):
        zero = jnp.zeros_like(own)
        return lax.psum(jnp.stack([jnp.where(col == b, own, zero) for b in range(2)]), "col")

    native[0], others[0] = mine, other
    theirs0 = exchange(other)
    if few_cols:
        down_raw = down(raw)
    sizes = [c for _, c in chunks]
    cut = sizes[1]
    mine1, others[1] = gather(1, sizes[1])
    chain.hold(others[1])
    (native[0],) = meet(mine, theirs0, width)
    (others[1],) = chain.passed
    hop(0)
    theirs1 = exchange(others[1])
    mine2, others[2] = gather(2, sizes[2])
    (native[1],) = meet(mine1, theirs1, sizes[1])
    hop(1)
    mine3, others[3] = gather(3, sizes[3])
    chain.hold(others[2], others[3])
    hop(0)
    others[2], others[3] = chain.passed
    theirs2, theirs3 = exchange(others[2]), exchange(others[3])
    put, keep = placement(chain, place, lands, cycles)
    hop(1)
    (native[2],) = meet(mine2, theirs2, sizes[2])
    hop(2)
    chain.hold(top)
    group(hop_part(0), meet_part(3, mine3, theirs3))
    (top,) = chain.passed
    top = lax.ppermute(top, "row", first_swap)
    if few_cols:
        side_raw = side(raw, down_raw)
    finish(0)
    (lead,) = chain.whole(
        lead_kernel, "lead", place, (x_mine[0], x_other[0]), [array(2, size, size)]
    )
    if few_cols:
        down_lead = down(lead)
    else:
        leads = from_two(lead)
    group(hop_part(2), both_part(1, 3))
    if few_cols:
        pieces = [raw, down_raw, side_raw]
    else:
        raws = from_two(raw)
        pieces = [raws[0], raws[1]]
    panels, panel_own, firsts = panel_rows(chain, place, onehot, pieces)
    tops = lax.ppermute(firsts, "row", first_swap)
    if few_cols:
        side_lead = side(lead, down_lead)
    if few_cols:
        panel_mine, panel_other = pair(lead, down_lead, side_lead, 2)
    else:
        panel_mine, panel_other = leads[:, 0], leads[:, 1]
    group(hop_part(2), hop_part(3), finish_part(1))
    side_rows, lower1, corner = factor_panels(
        chain, place, me, (panel_mine, panel_other), tops, panels, panel_own, put, keep
    )
    factors = (side_rows, keep, lower1, corner)

    def update(which, result):
        sets = [(native[i], others[i], x_mine[i], x_other[i]) for i in which]
        return update_columns(
            chain, place, me, matrix, sets, top, factors, chunks[which[0]][0], width, result
        )

    group(hop_part(3), finish_part(2))
    result = update((0, 1, 2), None)
    finish(3)
    result = update((3,), result)
    return result.transpose(0, 2, 1, 3)


def solution(mesh):
    return jax.shard_map(
        body,
        mesh=mesh,
        in_specs=(P(None, "row", None, "col"), P()),
        out_specs=P(None, "row", None, "col"),
        check_vma=False,
    )
```

```python
import functools

import jax
import jax.numpy as jnp
from jax import lax
from jax.experimental import pallas as pl
from jax.experimental.pallas import tpu as pltpu
from jax.sharding import PartitionSpec as P

STEPS = 2
NEWTON = 3
F32 = jnp.float32
BF16 = jnp.bfloat16
I32 = jnp.int32
VMEM_LIMIT = 24 * 1024 * 1024
CHEAP = pl.CostEstimate(flops=1024, bytes_accessed=1024, transcendentals=0)
ANY = pl.BlockSpec(memory_space=pl.ANY)
SMEM = pl.BlockSpec(memory_space=pltpu.SMEM)
VMEM = pl.BlockSpec(memory_space=pltpu.VMEM)


def dot(a, b):
    return jnp.dot(a, b, preferred_element_type=F32)


def dot_full(a, b):
    return jnp.dot(a, b, precision=lax.Precision.HIGHEST, preferred_element_type=F32)


def params():
    return pltpu.CompilerParams(vmem_limit_bytes=VMEM_LIMIT)


def iota(shape, dim):
    return lax.broadcasted_iota(I32, shape, dim)


def to_column(row):
    size = row.shape[1]
    diagonal = iota((size, size), 0) == iota((size, size), 1)
    return jnp.sum(jnp.where(diagonal, row.astype(F32), 0.0), axis=1, keepdims=True).astype(I32)


def to_row(column):
    size = column.shape[0]
    diagonal = iota((size, size), 0) == iota((size, size), 1)
    return jnp.sum(jnp.where(diagonal, column.astype(F32), 0.0), axis=0, keepdims=True).astype(I32)


def pick_sum(mask, value, axis):
    return jnp.sum(jnp.where(mask, value.astype(F32), 0.0), axis=axis, keepdims=True).astype(I32)


def start_kernel(
    rows, place, pivot_ref, matrix_ref, block_ref,
    onehot_ref, owner_ref, me_ref, lands_ref, raw_ref, mine_ref, other_ref, top_ref, token_ref, sem,
):
    copy = pltpu.make_async_copy(matrix_ref.at[0], top_ref, sem)
    copy.start()
    cycles, width, size, _ = block_ref.shape
    chip, core = place[0], place[1]
    row = 2 * chip + core

    @pl.when(pl.program_id(0) == 0)
    def _():
        square = (size, size)
        pivot0, pivot1 = pivot_ref[0:1], pivot_ref[1:2]
        column0 = to_column(pivot0)
        down, across = iota(square, 0), iota(square, 1)
        again = column0 == pivot1
        inner = column0 == across + size
        at = iota((1, size), 1)
        second = size + at + pick_sum(inner, down - across - size, 0)
        source1 = pivot1 + pick_sum(again, down - pivot1, 0)
        leaves0 = iota((size, 1), 0) + pick_sum(again, second - down, 1)
        device_of = lambda r: r // size % rows
        local_of = lambda r: r // (size * rows) * size + r % size

        def of_slots(source, leaves):
            device = device_of(source)
            owner = device // 2
            me = device == row
            come = jnp.where(jnp.logical_and(chip == 0, owner != 0), leaves, source)
            taken = jnp.where(device_of(come) == row, local_of(come), -1)
            return owner, me.astype(I32), taken

        first = of_slots(column0, leaves0)
        last = of_slots(to_column(source1), to_column(second))
        swapped = core == 1
        mine = [jnp.where(swapped, b, a) for a, b in zip(first, last)]
        other = [jnp.where(swapped, a, b) for a, b in zip(first, last)]
        for half, values in enumerate((mine, other)):
            owner_ref[half] = values[0]
            me_ref[half] = values[1]
            for cycle in range(cycles):
                hit = values[2] == across + cycle * size
                onehot_ref[half * size : (half + 1) * size, cycle * size : (cycle + 1) * size] = (
                    jnp.where(hit, 1.0, 0.0).astype(BF16)
                )

        slots = STEPS * size
        lands = []
        for source in (pivot0, source1):
            outside = jnp.logical_and(device_of(source) == row, source >= slots)
            lands.append(jnp.where(outside, local_of(source), -1))
        by_top = []
        leaving = (leaves0, to_column(second))
        landing = [to_column(v) for v in lands]
        for half in range(2):
            total = jnp.full((1, size), -1, I32)
            for leave, land in zip(leaving, landing):
                total += pick_sum(leave == across + half * size, land + 1, 0)
            by_top.append(total)
        lands = [jnp.where(chip == 0, a, b) for a, b in zip(by_top, lands)]
        lands_ref[0:1] = jnp.where(swapped, lands[1], lands[0])
        lands_ref[1:2] = jnp.where(swapped, lands[0], lands[1])
        raw_ref[...] = block_ref[:, 0]

    gather_step(onehot_ref, block_ref, mine_ref, other_ref)
    copy.wait()


def gather_step(onehot_ref, block_ref, mine_ref, other_ref):
    cycles, width, size, _ = block_ref.shape
    columns = [
        jnp.concatenate([block_ref[cycle, b] for cycle in range(cycles)], 0) for b in range(width)
    ]
    columns = columns[0] if width == 1 else jnp.concatenate(columns, 1)
    total = dot(onehot_ref[...], columns).astype(BF16)
    for b in range(width):
        mine_ref[b] = total[:size, b * size : (b + 1) * size]
        other_ref[b] = total[size:, b * size : (b + 1) * size]


def constant(shape):
    return pl.BlockSpec(
        shape, lambda *j, n=len(shape): (0,) * n, pipeline_mode=pl.Buffered(1)
    )


def array(*shape, dtype=BF16):
    return jax.ShapeDtypeStruct(shape, dtype)


TOKEN = array(8, 128, dtype=F32)


def start(place, pivots, matrix, width, rows):
    cycles, blocks, size, _ = matrix.shape
    slots = STEPS * size
    part = array(width, size, size)
    outs = [
        array(slots, cycles * size),
        array(2, size, 1, dtype=I32),
        array(2, size, 1, dtype=I32),
        array(2, size, dtype=I32),
        array(cycles, size, size),
        part,
        part,
    ]
    return pl.pallas_call(
        functools.partial(start_kernel, rows),
        grid=(1,),
        in_specs=[
            SMEM,
            constant(pivots.shape),
            ANY,
            pl.BlockSpec((cycles, width, size, size), lambda j: (0, 0, 0, 0)),
        ],
        out_specs=[constant(o.shape) for o in outs] + [ANY, ANY],
        out_shape=outs + [array(blocks, size, size), TOKEN],
        scratch_shapes=[pltpu.SemaphoreType.DMA],
        compiler_params=params(),
        cost_estimate=CHEAP,
        name="start",
    )(place, pivots, matrix, matrix)


class Chain:
    def __init__(self, token):
        self.token = token
        self.due = []
        self.held = []

    def hold(self, *arrays):
        self.held = list(arrays)

    def need(self, *arrays):
        self.due += arrays

    def run(self, kernel, name, operands, in_specs, out_shape, out_specs, **options):
        operands, in_specs = list(operands), list(in_specs)
        given, made = len(operands), len(out_shape)
        held, waits = self.held, [self.token, *self.due]
        self.due, self.held = [], []
        aliases = dict(options.pop("input_output_aliases", {}))
        for i in range(len(held)):
            aliases[given + len(waits) + i] = made + 1 + i
        passed = len(held)

        def inner(*refs):
            outs = given + len(waits) + passed
            kernel(*refs[:given], *refs[outs : outs + made], *refs[outs + made + 1 + passed :])

        outs = pl.pallas_call(
            inner,
            in_specs=in_specs + [ANY] * (len(waits) + passed),
            out_specs=list(out_specs) + [ANY] * (1 + passed),
            out_shape=list(out_shape) + [TOKEN] + [array(*a.shape) for a in held],
            input_output_aliases=aliases,
            compiler_params=params(),
            cost_estimate=CHEAP,
            name=name,
            **options,
        )(*operands, *waits, *held)
        self.token, self.passed = outs[made], outs[made + 1 :]
        return outs[:made]

    def whole(self, kernel, name, place, operands, out_shape, **options):
        return self.run(
            kernel,
            name,
            (place, *operands),
            [SMEM] + [VMEM] * len(operands),
            out_shape,
            [VMEM] * len(out_shape),
            **options,
        )


    def together(self, place, parts):
        def kernel(place_ref, *refs):
            at, made = 0, sum(len(part[1]) for part in parts)
            for part, operands, shapes in parts:
                part(place_ref, *refs[at : at + len(operands)], *refs[made : made + len(shapes)])
                at += len(operands)
                made += len(shapes)

        name = "_".join(getattr(part[0], "func", part[0]).__name__[:-7] for part in parts)
        outs = self.whole(
            kernel,
            name,
            place,
            [operand for part in parts for operand in part[1]],
            [shape for part in parts for shape in part[2]],
        )
        split, at = [], 0
        for part in parts:
            split.append(outs[at : at + len(part[2])])
            at += len(part[2])
        return split


def gather_rows(chain, matrix, onehot, first, count, width):
    cycles, _, size, _ = matrix.shape
    part = array(count, size, size)
    part_spec = pl.BlockSpec((width, size, size), lambda j: (j, 0, 0))
    return chain.run(
        gather_step,
        "gather_rows",
        (onehot, matrix),
        [
            VMEM,
            pl.BlockSpec((cycles, width, size, size), lambda j: (0, j + first // width, 0, 0)),
        ],
        [part, part],
        [part_spec, part_spec],
        grid=(count // width,),
    )


def meet_kernel(place, mine_ref, theirs_ref, *out_refs):
    at = 0
    for out_ref in out_refs:
        count = out_ref.shape[0]
        out_ref[...] = mine_ref[at : at + count] + theirs_ref[at : at + count]
        at += count


def meet_more_kernel(place, mine_ref, theirs_ref, extra_ref, out_ref):
    count = mine_ref.shape[0]
    out_ref[:count] = mine_ref[...] + theirs_ref[...]
    out_ref[count:] = extra_ref[...]


def lead_kernel(place, mine_ref, other_ref, out_ref):
    out_ref[0] = mine_ref[0]
    out_ref[1] = other_ref[0]


def merge_kernel(place, owner_ref, native_ref, received_ref, out_ref):
    own = jnp.logical_or(place[0] == 0, owner_ref[0] == place[0])
    for b in range(out_ref.shape[0]):
        out_ref[b] = jnp.where(own, native_ref[b], received_ref[b])


def merge_or_send_kernel(place, owner_ref, native_ref, received_ref, fresh_ref, out_ref, *, chips):
    own = jnp.logical_or(place[0] == 0, owner_ref[0] == place[0])
    end = jnp.logical_or(place[0] == 0, place[0] == chips - 1)
    for b in range(out_ref.shape[0]):
        merged = jnp.where(own, native_ref[b], received_ref[b])
        out_ref[b] = jnp.where(end, fresh_ref[b], merged)


def finish_kernel(place, owner_ref, me_ref, native_ref, *refs):
    *received, mine_ref, send_ref = refs
    chips = len(received) + 1
    chip = place[0]
    owner = owner_ref[0]
    me = me_ref[0] != 0
    passed = jnp.logical_and(owner == chip, chip != 0)
    passed_mine = jnp.logical_and(passed, me)
    passed_other = jnp.logical_and(passed, jnp.logical_not(me))
    for at in range(chips):

        @pl.when(chip == at)
        def _(at=at):
            for b in range(native_ref.shape[0]):
                native = native_ref[b]
                left = received[at - 1][b] if at > 0 else native
                right = received[chips - 2 - at][b] if at < chips - 1 else native
                new = jnp.where(owner < chip, left, jnp.where(owner > chip, right, native))
                mine_ref[b] = jnp.where(passed_mine, left, new)
                send_ref[b] = jnp.where(passed_other, left, new)


def side_kernel(place, own_ref, down_ref, out_ref):
    out_ref[...] = jnp.where(place[2] < 2, own_ref[...], down_ref[...])


def pair_kernel(place, own_ref, down_ref, side_ref, *out_refs):
    near = jnp.where(place[2] < 2, own_ref[...], down_ref[...])
    even = place[2] % 2 == 0
    first = jnp.where(even, near, side_ref[...])
    second = jnp.where(even, side_ref[...], near)
    for i, out_ref in enumerate(out_refs):
        out_ref[0] = first[i]
        out_ref[1] = second[i]


def placement_kernel(place, lands_ref, put_ref, keep_ref):
    cycles, size, slots = put_ref.shape
    for cycle in range(cycles):
        at = iota((size, size), 0) + cycle * size
        halves = []
        for half in range(2):
            hit = jnp.where(lands_ref[half : half + 1] == at, 1.0, 0.0)
            put_ref[cycle, :, half * size : (half + 1) * size] = hit.astype(BF16)
            halves.append(hit)
        filled = jnp.sum(halves[0] + halves[1], axis=1, keepdims=True)
        keep_ref[cycle] = jnp.broadcast_to(1.0 - filled, (size, size)).astype(BF16)


def placement(chain, place, lands, cycles):
    size = lands.shape[1]
    return chain.whole(
        placement_kernel,
        "placement",
        place,
        (lands,),
        [array(cycles, size, STEPS * size), array(cycles, size, size)],
    )


def three_parts(a):
    high = a.astype(BF16)
    rest = a - high.astype(F32)
    mid = rest.astype(BF16)
    low = (rest - mid.astype(F32)).astype(BF16)
    return jnp.concatenate([low, mid, high], 1)


def sum_parts(a):
    size = a.shape[1] // 3
    return (a[:, :size] + a[:, size : 2 * size]) + a[:, 2 * size :]


def newton_inverse(diag, identity):
    third = 1.0 / 3.0
    approx = (2.0 * identity - diag.astype(F32) * third) * third
    for _ in range(NEWTON - 1):
        product = sum_parts(dot(diag, three_parts(approx)))
        approx = dot_full(approx, 2.0 * identity - product)
    return approx


def whole_rows(place, me_ref, own_mine, own_other, x_mine, x_other):
    mine = jnp.where(me_ref[0] != 0, own_mine, x_mine)
    other = jnp.where(me_ref[1] != 0, own_other, x_other)
    first_core = place[1] == 0
    return jnp.where(first_core, mine, other), jnp.where(first_core, other, mine)


def old_rows(place, x_mine, x_other, top_mine, top_other):
    first_chip = place[0] == 0
    return jnp.concatenate(
        [
            jnp.where(first_chip, top_mine, x_mine),
            jnp.where(first_chip, top_other, x_other),
        ],
        axis=0,
    )


def panel_rows_kernel(place, onehot_ref, *rest):
    *pieces, raw_ref, own_ref, first_ref, sems = rest
    _, cycles, size, _ = raw_ref.shape

    def fetch(first, second):
        copies = [
            pltpu.make_async_copy(source, raw_ref.at[b], sems.at[b])
            for b, source in enumerate((first, second))
        ]
        for copy in copies:
            copy.start()
        for copy in copies:
            copy.wait()

    if len(pieces) == 2:
        fetch(*pieces)
    else:
        own, down, over = pieces
        for col, pair in enumerate(((own, over), (over, own), (down, over), (over, down))):

            @pl.when(place[2] == col)
            def _(pair=pair):
                fetch(*pair)

    flat = [raw_ref[b].reshape(cycles * size, size) for b in range(2)]
    total = dot(onehot_ref[...], jnp.concatenate(flat, 1)).astype(BF16)
    for b in range(2):
        own_ref[b] = total[:, b * size : (b + 1) * size]
        first_ref[b] = raw_ref[b, 0]


def panel_rows(chain, place, onehot, pieces):
    cycles, size, _ = pieces[0].shape
    return chain.run(
        panel_rows_kernel,
        "panel_rows",
        (place, onehot, *pieces),
        [SMEM, VMEM] + [ANY] * len(pieces),
        [
            array(2, cycles, size, size),
            array(2, STEPS * size, size),
            array(2, size, size),
        ],
        [VMEM] * 3,
        scratch_shapes=[pltpu.SemaphoreType.DMA((2,))],
    )


def panel_kernel(
    place, me_ref, xm_ref, xo_ref, top_ref, raw_ref, own_ref, put_ref, keep_ref,
    side_ref, lower1_ref, corner_ref,
):
    _, cycles, size, _ = raw_ref.shape
    row = 2 * place[0] + place[1]
    slots = STEPS * size
    raw0, raw1 = raw_ref.at[0], raw_ref.at[1]
    new0, new1, old = [], [], []
    for b in range(2):
        mine, other = own_ref[b, :size], own_ref[b, size:]
        upper, below = whole_rows(place, me_ref, mine, other, xm_ref[b], xo_ref[b])
        new0.append(upper)
        new1.append(below)
        old.append(old_rows(place, xm_ref[b], xo_ref[b], raw_ref[b, 0], top_ref[b]))
    old = jnp.concatenate(old, 1)
    identity = jnp.where(iota((size, size), 0) == iota((size, size), 1), 1.0, 0.0).astype(F32)
    inverse0 = three_parts(newton_inverse(new0[0], identity))
    corner = sum_parts(dot(new1[0], inverse0)).astype(BF16)
    corner_ref[...] = corner
    inverse1 = three_parts(
        newton_inverse((new1[1].astype(F32) - dot(corner, new0[1])).astype(BF16), identity)
    )
    for cycle in range(cycles):
        put = put_ref[cycle]
        keep = keep_ref[cycle]
        both = dot(put, old)
        left = (both[:, :size] + (keep * raw0[cycle]).astype(F32)).astype(BF16)
        right = both[:, size:] + (keep * raw1[cycle]).astype(F32)
        if cycle == 0:
            left = jnp.where(row == 0, new0[0], jnp.where(row == 1, new1[0], left))
            right = jnp.where(
                row == 0, new0[1].astype(F32), jnp.where(row == 1, new1[1].astype(F32), right)
            )
        lower = sum_parts(dot(left, inverse0))
        if cycle == 0:
            lower = jnp.where(row == 0, 0.0, lower)
        lower = lower.astype(BF16)
        side_ref[cycle, :, :slots] = put
        side_ref[cycle, :, slots:] = -lower
        right = (right - dot(lower, new0[1])).astype(BF16)
        lower = sum_parts(dot(right, inverse1))
        if cycle == 0:
            lower = jnp.where(row <= 1, 0.0, lower)
        lower1_ref[cycle] = lower.astype(BF16)


def factor_panels(chain, place, me, rows, tops, raw, own, put, keep):
    cycles, size, _ = keep.shape
    return chain.run(
        panel_kernel,
        "factor_panels",
        (place, me, *rows, tops, raw, own, put, keep),
        [SMEM] + [VMEM] * 8,
        [
            array(cycles, size, (STEPS + 1) * size),
            array(cycles, size, size),
            array(size, size),
        ],
        [VMEM] * 3,
    )


def update_kernel(first, counts, place, me_ref, block_ref, top_ref, *rest):
    sets = [rest[4 * i : 4 * i + 4] for i in range(len(counts))]
    side_ref, keep_ref, lower1_ref, corner_ref = rest[4 * len(counts) : 4 * len(counts) + 4]
    out_ref, both_ref, below_ref = rest[-3:]
    cycles, width, size, _ = block_ref.shape
    at = pl.program_id(0) * width
    row = 2 * place[0] + place[1]
    slots = STEPS * size
    start = 0
    for (native_ref, own_ref, xm_ref, xo_ref), count in zip(sets, counts):

        def prepare(start=start, native_ref=native_ref, own_ref=own_ref, xm_ref=xm_ref, xo_ref=xo_ref):
            for b in range(width):
                i = at + (b - start)
                xm, xo = xm_ref[i], xo_ref[i]
                upper, below = whole_rows(place, me_ref, native_ref[i], own_ref[i], xm, xo)
                old = old_rows(place, xm, xo, block_ref[0, b], top_ref[b])
                part = slice(b * size, (b + 1) * size)
                both_ref[:slots, part] = old
                both_ref[slots:, part] = upper
                below_ref[:, part] = below

        if len(counts) == 1:
            prepare()
        else:
            pl.when(jnp.logical_and(at >= start, at < start + count))(prepare)
        start += count
    join = lambda parts: parts[0] if width == 1 else jnp.concatenate(parts, 1)
    both = both_ref[...]
    upper = both[slots:]
    upper1 = (below_ref[...].astype(F32) - dot(corner_ref[...], upper)).astype(BF16)
    for cycle in range(cycles):
        keep = keep_ref[cycle]
        kept = join([block_ref[cycle, b] * keep for b in range(width)])
        block = (dot(side_ref[cycle], both) + kept.astype(F32)).astype(BF16)
        if cycle == 0:
            block = jnp.where(row == 0, upper, jnp.where(row == 1, upper1, block))
        block = (block.astype(F32) - dot(lower1_ref[cycle], upper1)).astype(BF16)
        for b in range(width):
            out_ref[cycle, b] = block[:, b * size : (b + 1) * size]
    if first == 0:

        @pl.when(jnp.logical_and(pl.program_id(0) == 0, place[2] == 0))
        def _():
            for cycle in range(cycles):
                block = -side_ref[cycle, :, slots:]
                if cycle == 0:
                    block = jnp.where(row == 0, upper[:, :size], block)
                out_ref[cycle, 0] = block

        @pl.when(jnp.logical_and(pl.program_id(0) == 0, place[2] == 1))
        def _():
            for cycle in range(cycles):
                block = lower1_ref[cycle]
                if cycle == 0:
                    block = jnp.where(
                        row == 0, upper[:, :size], jnp.where(row == 1, upper1[:, :size], block)
                    )
                out_ref[cycle, 0] = block


def update_columns(chain, place, me, matrix, sets, top, factors, first, width, result):
    cycles, blocks, size, _ = matrix.shape
    counts = [s[0].shape[0] for s in sets]
    rows = [r for s in sets for r in s]
    at = lambda j: j + first // width
    blocks_spec = pl.BlockSpec((cycles, width, size, size), lambda j: (0, at(j), 0, 0))
    top_spec = pl.BlockSpec((width, size, size), lambda j: (at(j), 0, 0))
    operands = [place, me, matrix, top, *rows, *factors]
    in_specs = [SMEM, VMEM, blocks_spec, top_spec]
    in_specs += [VMEM] * (len(rows) + len(factors))
    aliases = {}
    if result is not None:
        aliases = {len(operands): 0}
        operands.append(result)
        in_specs.append(ANY)
    return chain.run(
        functools.partial(update_kernel, first, counts),
        "update_columns",
        operands,
        in_specs,
        [array(*matrix.shape)],
        [blocks_spec],
        grid=(sum(counts) // width,),
        scratch_shapes=[
            pltpu.VMEM(((STEPS + 1) * size, width * size), BF16),
            pltpu.VMEM((size, width * size), BF16),
        ],
        input_output_aliases=aliases,
    )[0]


def split_blocks(blocks):
    width = 2 if blocks % 2 == 0 else 1
    base, extra = divmod(blocks // width - 1, 3)
    counts = [width] + [width * (base + (1 if i < extra else 0)) for i in range(3)]
    return width, [(sum(counts[:i]), c) for i, c in enumerate(counts)]


def body(matrix, pivots):
    rows = lax.axis_size("row")
    cols = lax.axis_size("col")
    chips = rows // 2
    row = lax.axis_index("row")
    col = lax.axis_index("col")
    cycles, size, blocks, _ = matrix.shape
    plain = matrix.transpose(0, 2, 1, 3)
    matrix = pltpu.with_memory_space_constraint(plain, pltpu.HBM)
    place = jnp.stack([row // 2, row % 2, col]).astype(I32)
    width, chunks = split_blocks(blocks)
    count = len(chunks)
    few_cols = cols == 4

    swap = [(r, r ^ 1) for r in range(rows)]
    first_swap = [(0, 1), (1, 0)]
    down_pairs = [(0, 2), (1, 3)]
    side_pairs = [(0, 1), (1, 0), (2, 3), (3, 2)]

    def hop_pairs(h):
        pairs = []
        for a, b in ((h, h + 1), (chips - 1 - h, chips - 2 - h)):
            pairs += [(2 * a, 2 * b), (2 * a + 1, 2 * b + 1)]
        return pairs

    onehot, owner, me, lands, raw, mine, other, top, token = start(
        place, pivots, matrix, width, rows
    )
    chain = Chain(token)
    native, others, x_mine, x_send, x_other = {}, {}, {}, {}, {}
    hops = {i: [] for i in range(count)}

    def exchange(own):
        return lax.ppermute(own, "row", swap)

    def gather(i, blocks):
        return gather_rows(chain, matrix, onehot, chunks[i][0], blocks, width)

    def meet(mine, theirs, *counts):
        return chain.whole(
            meet_kernel, "meet", place, (mine, theirs), [array(c, size, size) for c in counts]
        )

    def hop_part(i):
        h = len(hops[i])
        shape = array(*native[i].shape)

        def go(out):
            hops[i].append(lax.ppermute(out[0], "row", hop_pairs(h)))

        return merge_kernel, (owner, native[i], hops[i][-1]), [shape], go

    def both_part(i, j):
        if chips != 4 or native[i].shape != native[j].shape:
            hop(j)
            return hop_part(i)

        def go(out):
            arrived = lax.ppermute(out[0], "row", hop_pairs(0) + hop_pairs(2))
            hops[i].append(arrived)
            hops[j].append(arrived)

        kernel = functools.partial(merge_or_send_kernel, chips=chips)
        operands = (owner, native[i], hops[i][-1], native[j])
        return kernel, operands, [array(*native[i].shape)], go

    def finish_part(i):
        while len(hops[i]) < chips - 1:
            hop(i)

        def go(out):
            x_mine[i], x_send[i] = out
            x_other[i] = exchange(x_send[i])

        operands = (owner, me, native[i], *hops[i])
        return finish_kernel, operands, [array(*native[i].shape)] * 2, go

    def meet_part(i, mine, theirs):
        def go(out):
            (native[i],) = out

        return meet_kernel, (mine, theirs), [array(*mine.shape)], go

    def group(*parts):
        outs = chain.together(place, [part[:3] for part in parts])
        for part, out in zip(parts, outs):
            part[3](out)

    def hop(i):
        if hops[i]:
            group(hop_part(i))
        else:
            hops[i].append(lax.ppermute(native[i], "row", hop_pairs(0)))

    def finish(i):
        group(finish_part(i))

    def side(own, down):
        (out,) = chain.whole(side_kernel, "side", place, (own, down), [array(*own.shape)])
        return lax.ppermute(out, "col", side_pairs)

    def down(own):
        return lax.ppermute(own, "col", down_pairs)

    def pair(own, down, side, made):
        return chain.whole(
            pair_kernel, "pair", place, (own, down, side), [array(2, size, size)] * made
        )

    def from_two(own):
        zero = jnp.zeros_like(own)
        return lax.psum(jnp.stack([jnp.where(col == b, own, zero) for b in range(2)]), "col")

    native[0], others[0] = mine, other
    theirs0 = exchange(other)
    if few_cols:
        down_raw = down(raw)
    sizes = [c for _, c in chunks]
    cut = sizes[1]
    mine1, others[1] = gather(1, sizes[1])
    chain.hold(others[1])
    (native[0],) = meet(mine, theirs0, width)
    (others[1],) = chain.passed
    hop(0)
    theirs1 = exchange(others[1])
    (native[1],) = meet(mine1, theirs1, sizes[1])
    hop(1)
    mine2, others[2] = gather(2, sizes[2])
    mine3, others[3] = gather(3, sizes[3])
    chain.hold(others[2], others[3])
    hop(0)
    others[2], others[3] = chain.passed
    theirs2, theirs3 = exchange(others[2]), exchange(others[3])
    put, keep = placement(chain, place, lands, cycles)
    hop(1)
    (native[2],) = meet(mine2, theirs2, sizes[2])
    hop(2)
    chain.hold(top)
    group(hop_part(0), meet_part(3, mine3, theirs3))
    (top,) = chain.passed
    top = lax.ppermute(top, "row", first_swap)
    if few_cols:
        side_raw = side(raw, down_raw)
    finish(0)
    (lead,) = chain.whole(
        lead_kernel, "lead", place, (x_mine[0], x_other[0]), [array(2, size, size)]
    )
    if few_cols:
        down_lead = down(lead)
    else:
        leads = from_two(lead)
    group(hop_part(2), both_part(1, 3))
    if few_cols:
        pieces = [raw, down_raw, side_raw]
    else:
        raws = from_two(raw)
        pieces = [raws[0], raws[1]]
    panels, panel_own, firsts = panel_rows(chain, place, onehot, pieces)
    tops = lax.ppermute(firsts, "row", first_swap)
    if few_cols:
        side_lead = side(lead, down_lead)
    if few_cols:
        panel_mine, panel_other = pair(lead, down_lead, side_lead, 2)
    else:
        panel_mine, panel_other = leads[:, 0], leads[:, 1]
    group(hop_part(2), hop_part(3), finish_part(1))
    side_rows, lower1, corner = factor_panels(
        chain, place, me, (panel_mine, panel_other), tops, panels, panel_own, put, keep
    )
    factors = (side_rows, keep, lower1, corner)

    def update(which, result):
        sets = [(native[i], others[i], x_mine[i], x_other[i]) for i in which]
        return update_columns(
            chain, place, me, matrix, sets, top, factors, chunks[which[0]][0], width, result
        )

    group(hop_part(3), finish_part(2))
    result = update((0, 1, 2), None)
    finish(3)
    result = update((3,), result)
    return result.transpose(0, 2, 1, 3)


def solution(mesh):
    return jax.shard_map(
        body,
        mesh=mesh,
        in_specs=(P(None, "row", None, "col"), P()),
        out_specs=P(None, "row", None, "col"),
        check_vma=False,
    )
```
